256 devices in a mesh: pos: 16 (over z, core), ty: 4 (over x), tx: 4 (over y).
Axes of the slice: x: 4, y: 4, z: 8, core: 2. Of those that a mesh axis runs over, the one named last changes fastest.
Arguments:
- object_field: float32 [2, 1536, 1536], P(None, 'ty', 'tx'), may hold values from -5 to 5
- probe: float32 [4, 2, 256, 256], replicated, may hold values from -4 to 4
- amplitudes: float32 [512, 256, 256], P(('pos', 'ty', 'tx')), may hold values from 0.5 to 4
- live_pixels: int32 [256, 256], replicated, may hold values 0 or 1
- offsets: int32 [512, 2], P(('pos', 'ty', 'tx')), may hold values from 0 to 1280, as said below
Outputs:
- object_new: float32 [2, 1536, 1536], P(None, 'ty', 'tx')
- probe_new: float32 [4, 2, 256, 256], replicated
The draws below stay inside these ranges and needn't reach their ends.
Inputs may be any that keep to these rules, and one draw needn't show every extreme that they name: The position of row b of offsets starts inside object tile (((b // 2) // 4) % 4, (b // 2) % 4) of 384 x 384 pixels, and its whole window lies inside the object.
All inputs are finite; a program needn't handle non-finite values.
Results may differ from the reference program's by a relative error of at most 0.0001.
Values sent between devices are 32-bit elements; how exact they have to be, the bound alone decides.
A program may use at most 64 MiB of HBM per device.

```python
import math
import jax
import jax.numpy as jnp
from jax import lax

P_SIZE = 256
MODES = 4
OT = 384
POS_DEV = 2
NOY = 1536
NOX = 1536
B = 512
N_TY = 4
N_TX = 4


def draw_offsets(key, part):
    key = jax.random.fold_in(key, 11)
    key_row, key_col = jax.random.split(key)
    owner = jnp.arange(B, dtype=jnp.int32) // POS_DEV
    tile_row = owner // N_TX % N_TY
    tile_col = owner % N_TX
    span_row = jnp.minimum(OT, NOY - P_SIZE - tile_row * OT + 1)
    span_col = jnp.minimum(OT, NOX - P_SIZE - tile_col * OT + 1)
    rows = tile_row * OT + jax.random.randint(key_row, (B,), 0, span_row)
    cols = tile_col * OT + jax.random.randint(key_col, (B,), 0, span_col)
    slots = jnp.arange(B, dtype=jnp.int32)
    rows = jnp.where(slots == B - 1, NOY - P_SIZE, jnp.where(slots == 0, 0, rows))
    cols = jnp.where(slots == B - 1, NOX - P_SIZE, jnp.where(slots == 0, 0, cols))
    return jnp.stack([rows, cols], axis=1).astype(jnp.int32)


def plant(values, rng, smallest, top_value):
    place = [jax.random.randint(jax.random.fold_in(rng, axis), (), 0, length) for axis, length in enumerate(values.shape)]
    widest = values.shape.index(max(values.shape))
    beside = place[:widest] + [(place[widest] + 1) % values.shape[widest]] + place[widest + 1:]
    return values.at[tuple(place)].set(smallest).at[tuple(beside)].set(top_value)


def block_levels(key, extent, cuts, low, top_value):
    gain = 1.0
    for dim, shards_of in cuts:
        draws = jax.random.uniform(jax.random.fold_in(jax.random.fold_in(key, 6), dim), (shards_of,), jnp.float32, low / len(cuts), top_value / len(cuts))
        gain = gain * jnp.repeat(jnp.exp(draws), extent[dim] // shards_of).reshape((-1,) + (1,) * (len(extent) - 1 - dim))
    return gain


def scatter_about(stream_key, dims, spread, bound, pieces=(), kind=jnp.bfloat16):
    factor_of = block_levels(stream_key, dims, pieces, -0.22, 0.18) if pieces else 1.0
    values = jax.random.normal(stream_key, dims, jnp.float32) * spread * factor_of
    return jnp.minimum(jnp.maximum(values, -bound), bound).astype(kind)


def setup_inputs(seed: int = 0) -> dict:
    arg_keys = jax.random.split(jax.random.key(seed), 6)
    object_field = scatter_about(arg_keys[0], (2, NOY, NOX), 0.7, 5.0, ((1, 4), (2, 4)), jnp.float32)
    probe = scatter_about(arg_keys[1], (MODES, 2, P_SIZE, P_SIZE), 0.5, 4.0, (), jnp.float32)
    amplitudes = jnp.clip(jnp.exp(math.log(4.0) - 2.0794415 * jax.random.uniform(arg_keys[2], (B, P_SIZE, P_SIZE), jnp.float32) ** block_levels(arg_keys[2], (B, P_SIZE, P_SIZE), ((0, 256),), -0.2, 0.2)), 0.5, 4.0)
    live_pixels = plant((jax.random.randint(arg_keys[3], (P_SIZE, P_SIZE), 0, 32) < 31).astype(jnp.int32), jax.random.fold_in(arg_keys[3], 1), 0, 1)
    offsets = draw_offsets(jax.random.fold_in(arg_keys[5], 71), 0)
    return dict(object_field=object_field, probe=probe, amplitudes=amplitudes, live_pixels=live_pixels, offsets=offsets)


intensity_floor = 0.25
flux_floor = 0.25
tv_weight = 0.1

def reference(object_field, probe, amplitudes, live_pixels, offsets):
    probe_real = probe[:, 0]
    probe_imag = probe[:, 1]
    live = live_pixels == 1
    zero_index = jnp.zeros((), jnp.int32)

    def visit(slot_index, carry):
        accum, numer, denom = carry
        row = offsets[slot_index, 0].astype(jnp.int32)
        col = offsets[slot_index, 1].astype(jnp.int32)
        patch = lax.dynamic_slice(object_field, (zero_index, row, col), (2, P_SIZE, P_SIZE))
        patch_real = patch[0]
        patch_imag = patch[1]
        wave_real = probe_real * patch_real - probe_imag * patch_imag
        wave_imag = probe_real * patch_imag + probe_imag * patch_real
        far = jnp.fft.fft2(lax.complex(wave_real, wave_imag), norm='ortho')
        intensity = lax.optimization_barrier(jnp.sum(far.real * far.real + far.imag * far.imag, axis=0))
        factor = jnp.where(live, amplitudes[slot_index] / jnp.sqrt(jnp.maximum(intensity, intensity_floor)), 1.0)
        near = jnp.fft.ifft2(far * factor, norm='ortho')
        delta_real = near.real - wave_real
        delta_imag = near.imag - wave_imag
        grad_real = lax.optimization_barrier(jnp.sum(probe_real * delta_real + probe_imag * delta_imag, axis=0))
        grad_imag = lax.optimization_barrier(jnp.sum(probe_real * delta_imag - probe_imag * delta_real, axis=0))
        weight = lax.optimization_barrier(jnp.sum(probe_real * probe_real + probe_imag * probe_imag, axis=0))
        terms = jnp.stack([grad_real, grad_imag, weight]).astype(accum.dtype)
        region = lax.dynamic_slice(accum, (zero_index, row, col), (3, P_SIZE, P_SIZE))
        accum = lax.dynamic_update_slice(accum, region + terms, (zero_index, row, col))
        numer = numer + jnp.stack([patch_real * delta_real + patch_imag * delta_imag, patch_real * delta_imag - patch_imag * delta_real], axis=1).astype(numer.dtype)
        denom = denom + patch_real * patch_real + patch_imag * patch_imag
        return (accum, numer, denom)
    accum0 = jnp.zeros((3, NOY, NOX), object_field.dtype)
    numer0 = jnp.zeros_like(probe)
    denom0 = jnp.zeros((P_SIZE, P_SIZE), probe.dtype)
    accum, numer, denom = lax.fori_loop(0, B, visit, (accum0, numer0, denom0))
    probe_new = probe + numer / (denom + 1.0)
    updated = object_field + accum[:2] / (accum[2] + 1.0)
    padded = jnp.pad(updated, ((0, 0), (1, 1), (1, 1)))
    base = padded[:, :NOY + 1, :NOX + 1]
    flux_x = padded[:, :NOY + 1, 1:NOX + 2] - base
    flux_y = padded[:, 1:NOY + 2, :NOX + 1] - base
    magnitude = jnp.sqrt(jnp.maximum(lax.optimization_barrier(jnp.sum(flux_x * flux_x + flux_y * flux_y, axis=0)), flux_floor))
    norm_x = flux_x / magnitude
    norm_y = flux_y / magnitude
    divergence = norm_x[:, 1:, 1:] - norm_x[:, 1:, :-1] + norm_y[:, 1:, 1:] - norm_y[:, :-1, 1:]
    object_new = updated + tv_weight * divergence
    return (object_new, probe_new)
```

```python
import functools, math
import numpy as np, ml_dtypes
import jax, jax.numpy as jnp
from jax import lax
from jax.experimental import pallas as pl
from jax.experimental.pallas import tpu as pltpu
from jax.sharding import PartitionSpec as P

N = 256
H = 128
TILE = 384
EXT = 640
intensity_floor = 0.25
flux_floor = 0.25
tv_weight = 0.1
N_POS, N_Y, N_X = 16, 4, 4
f32, bf16 = jnp.float32, jnp.bfloat16


def tables():
    k = np.arange(H)
    ang = 2.0 * np.pi * ((k[:, None] * k[None, :]) % H) / H
    c, s = np.cos(ang) / 16.0, np.sin(ang) / 16.0
    m = np.block([[c, -s], [s, c]]).astype(np.float32)
    hi = m.astype(ml_dtypes.bfloat16)
    lo = (m - hi.astype(np.float32)).astype(ml_dtypes.bfloat16)
    fwd_right = np.concatenate([hi, hi, lo], 0)
    inv_right = np.concatenate([hi.T, hi.T, lo.T], 0)
    fwd_left = np.concatenate([hi.T, hi.T, lo.T], 1)
    inv_left = np.concatenate([hi, hi, lo], 1)
    th = 2.0 * np.pi * k / N
    tw = np.stack([np.cos(th), np.sin(th)]).astype(np.float32)
    lane_tw = np.stack([np.tile(tw[0], (8, 1)), np.tile(tw[1], (8, 1))])
    row_tw = np.stack([np.tile(tw[0][:, None], (1, H)), np.tile(tw[1][:, None], (1, H))])
    perm = np.concatenate([np.arange(0, N, 2), np.arange(1, N, 2)])
    pick = np.zeros((N, N), np.float32)
    pick[np.arange(N), perm] = 1.0
    pick = pick.astype(ml_dtypes.bfloat16)
    return fwd_right, inv_right, fwd_left, inv_left, lane_tw, row_tw, pick, pick.T.copy()


def split(x):
    hi = x.astype(bf16)
    lo = (x - hi.astype(f32)).astype(bf16)
    return hi, lo


def right(x, table):
    hi, lo = split(x)
    return jnp.dot(jnp.concatenate([hi, lo, hi], 1), table, preferred_element_type=f32)


def left(table, x):
    hi, lo = split(x)
    return jnp.dot(table, jnp.concatenate([hi, lo, hi], 0), preferred_element_type=f32)


def split_dot_l(p, x):
    hi, lo = split(x)
    return jnp.dot(p, hi, preferred_element_type=f32) + jnp.dot(p, lo, preferred_element_type=f32)


def split_dot_r(x, p):
    hi, lo = split(x)
    return jnp.dot(hi, p, preferred_element_type=f32) + jnp.dot(lo, p, preferred_element_type=f32)


def shift_up_left(x, srow, scol):
    lane = lax.broadcasted_iota(jnp.int32, (N + 8, 128), 1)
    back = lax.rem(128 - scol, 128)
    turned = [pltpu.roll(x[:, 128 * i:128 * (i + 1)], back, 1) for i in range(3)]
    keep = lane < 128 - scol
    x = jnp.concatenate([jnp.where(keep, turned[i], turned[i + 1]) for i in range(2)], 1)
    x = x.reshape(N // 8 + 1, 8, N)
    x = pltpu.roll(x, lax.rem(8 - srow, 8), 1)
    sub = lax.broadcasted_iota(jnp.int32, (N // 8, 8, N), 1)
    return jnp.where(sub < 8 - srow, x[:-1], x[1:]).reshape(N, N)


def shift_down_right(x, srow, scol):
    x = pltpu.roll(x.reshape(N // 8, 8, N), srow, 1)
    none = jnp.zeros((1, 8, N), f32)
    sub = lax.broadcasted_iota(jnp.int32, (N // 8 + 1, 8, N), 1)
    x = jnp.where(sub >= srow, jnp.concatenate([x, none], 0), jnp.concatenate([none, x], 0))
    x = x.reshape(N + 8, N)
    lane = lax.broadcasted_iota(jnp.int32, (N + 8, 128), 1)
    t = [pltpu.roll(x[:, 128 * i:128 * (i + 1)], scol, 1) for i in range(2)]
    keep = lane >= scol
    return jnp.concatenate([jnp.where(keep, t[0], 0.0), jnp.where(keep, t[1], t[0]), jnp.where(keep, 0.0, t[1])], 1)


def compute_kernel(slots, offs, ext, probe, amps, live, fr, ir, fl, il, ltw, rtw, pick, pick_t,
                   frame, sums,
                   patch, far, fac, grad, weight, mask):
    modes = probe.shape[0]
    frame[...] = jnp.zeros_like(frame)
    sums[...] = jnp.zeros_like(sums)
    w = jnp.zeros((N, N), f32)
    for m in range(modes):
        w = w + (probe[m, 0] * probe[m, 0] + probe[m, 1] * probe[m, 1])
    weight[...] = w
    on = (live[...] == 1).astype(bf16)
    on = jnp.dot(pick[...], on, preferred_element_type=f32).astype(bf16)
    mask[...] = jnp.dot(on, pick_t[...], preferred_element_type=f32)

    @pl.loop(0, slots)
    def _(p):
        row, col = offs[p, 0], offs[p, 1]
        row8, col128 = row // 8, col // 128
        srow, scol = row - row8 * 8, col - col128 * 128
        rows = pl.ds(pl.multiple_of(row8 * 8, 8), N + 8)
        cols = pl.ds(pl.multiple_of(col128 * 128, 128), N + 128)
        for c in range(2):
            patch[c] = shift_up_left(ext[c, rows, cols], srow, scol)
        pr, pi = patch[0], patch[1]
        sums[2 * modes] += pr * pr + pi * pi
        grad[...] = jnp.zeros_like(grad)
        fac[...] = jnp.zeros_like(fac)

        @pl.loop(0, modes, unroll=4)
        def _(m):
            pr, pi = patch[0], patch[1]
            qr, qi = probe[m, 0], probe[m, 1]
            wr = qr * pr - qi * pi
            wi = qr * pi + qi * pr
            ar, ai = wr[:, :H] + wr[:, H:], wi[:, :H] + wi[:, H:]
            br, bi = wr[:, :H] - wr[:, H:], wi[:, :H] - wi[:, H:]
            tc, ts = ltw[0, 0:1], ltw[1, 0:1]
            br, bi = br * tc + bi * ts, bi * tc - br * ts
            even = right(jnp.concatenate([ar, ai], 1), fr[...])
            odd = right(jnp.concatenate([br, bi], 1), fr[...])
            total = None
            rc, rs = rtw[0], rtw[1]
            for h, z in enumerate((even, odd)):
                zr, zi = z[:, :H], z[:, H:]
                ar, ai = zr[:H] + zr[H:], zi[:H] + zi[H:]
                br, bi = zr[:H] - zr[H:], zi[:H] - zi[H:]
                br, bi = br * rc + bi * rs, bi * rc - br * rs
                both = jnp.concatenate([jnp.concatenate([ar, br], 1), jnp.concatenate([ai, bi], 1)], 0)
                out = left(fl[...], both)
                far[m, h] = out
                sq = out * out
                power = sq[:H] + sq[H:]
                fac[h] += power

        amp = split_dot_r(split_dot_l(pick[...], amps[p]), pick_t[...])
        for h in range(2):
            want = jnp.concatenate([amp[:H, h * H:(h + 1) * H], amp[H:, h * H:(h + 1) * H]], 1)
            lv = jnp.concatenate([mask[:H, h * H:(h + 1) * H], mask[H:, h * H:(h + 1) * H]], 1)
            fac[h] = jnp.where(lv > 0.5, want * lax.rsqrt(jnp.maximum(fac[h], intensity_floor)), 1.0)

        @pl.loop(0, modes, unroll=4)
        def _(m):
            rc, rs = rtw[0], rtw[1]
            halves = []
            for h in range(2):
                f = far[m, h]
                k = fac[h]
                y = jnp.concatenate([f[:H] * k, f[H:] * k], 0)
                x = left(il[...], y)
                er, orr = x[:H, :H], x[:H, H:]
                ei, oi = x[H:, :H], x[H:, H:]
                orr, oi = orr * rc - oi * rs, oi * rc + orr * rs
                top = jnp.concatenate([er + orr, ei + oi], 1)
                bottom = jnp.concatenate([er - orr, ei - oi], 1)
                halves.append(right(jnp.concatenate([top, bottom], 0), ir[...]))
            e, o = halves
            er, ei, orr, oi = e[:, :H], e[:, H:], o[:, :H], o[:, H:]
            tc, ts = ltw[0, 0:1], ltw[1, 0:1]
            orr, oi = orr * tc - oi * ts, oi * tc + orr * ts
            nr = jnp.concatenate([er + orr, er - orr], 1)
            ni = jnp.concatenate([ei + oi, ei - oi], 1)
            pr, pi = patch[0], patch[1]
            qr, qi = probe[m, 0], probe[m, 1]
            dr = nr - (qr * pr - qi * pi)
            di = ni - (qr * pi + qi * pr)
            grad[0] += qr * dr + qi * di
            grad[1] += qr * di - qi * dr
            sums[2 * m] += pr * dr + pi * di
            sums[2 * m + 1] += pr * di - pi * dr

        for c in range(frame.shape[0]):
            frame[c, rows, cols] += shift_down_right(grad[c] if c < 2 else weight[...], srow, scol)


def compute_call(offs, ext, probe, amps, live, channels=3):
    slots = amps.shape[0]
    modes = probe.shape[0]
    vm = pl.BlockSpec(memory_space=pltpu.VMEM)
    consts = [jnp.asarray(t) for t in tables()]
    return pl.pallas_call(
        functools.partial(compute_kernel, slots),
        out_shape=(
            jax.ShapeDtypeStruct((channels, EXT, EXT), f32),
            jax.ShapeDtypeStruct((2 * modes + 1, N, N), f32),
        ),
        in_specs=[pl.BlockSpec(memory_space=pltpu.SMEM)] + [vm] * (4 + len(consts)),
        out_specs=(vm, vm),
        scratch_shapes=[
            pltpu.VMEM((2, N, N), f32),
            pltpu.VMEM((modes, 2, N, N), f32),
            pltpu.VMEM((2, H, N), f32),
            pltpu.VMEM((2, N, N), f32),
            pltpu.VMEM((N, N), f32),
            pltpu.VMEM((N, N), f32),
        ],
        compiler_params=pltpu.CompilerParams(vmem_limit_bytes=50 * 2**20),
        name="positions",
    )(offs, ext, probe, amps, live, *consts)


MESH = pl.DeviceIdType.MESH


class Wires:
    def __init__(self, send, recv):
        self.send, self.recv, self.count, self.started = send, recv, 0, []

    def slot(self):
        self.count += 1
        return self.count - 1

    def copy(self, src, dst, slot, to):
        return pltpu.make_async_remote_copy(
            src_ref=src, dst_ref=dst, send_sem=self.send.at[slot], recv_sem=self.recv.at[slot],
            device_id=to, device_id_type=MESH)

    def start(self, src, dst, slot, to):
        made = self.copy(src, dst, slot, to)
        made.start()
        self.started.append(made)
        return made

    def finish(self):
        for made in self.started:
            made.wait_send()


def greet(partners):
    barrier = pltpu.get_barrier_semaphore()
    for to in partners:
        pl.semaphore_signal(barrier, inc=1, device_id=to, device_id_type=MESH)
    pl.semaphore_wait(barrier, len(partners))


def places():
    p = lax.axis_index("pos")
    return p, p // 2, lax.rem(p, 2), lax.axis_index("ty"), lax.axis_index("tx")


def halo_kernel(obj, ext, here, send, recv):
    p, z, c, a, b = places()
    tile = obj.shape[1]
    up, down = lax.rem(a + N_Y - 1, N_Y), lax.rem(a + 1, N_Y)
    left, right_ = lax.rem(b + N_X - 1, N_X), lax.rem(b + 1, N_X)
    sib = {"pos": 2 * z + 1 - c}
    greet([sib, {"tx": left}, {"tx": right_}, {"ty": up}, {"ty": down},
           {"ty": up, "tx": left}, {"ty": down, "tx": right_}])
    w = Wires(send, recv)
    own = pltpu.make_async_copy(obj, ext.at[:, 0:tile, 0:tile], here)
    own.start()
    parts = [
        (obj.at[c, 0:N, 0:N], (pl.ds(tile, N), pl.ds(tile, N)), {"ty": up, "tx": left}),
        (obj.at[c, :, 0:N], (pl.ds(0, tile), pl.ds(tile, N)), {"tx": left}),
        (obj.at[c, 0:N, :], (pl.ds(tile, N), pl.ds(0, tile)), {"ty": up}),
    ]
    got = []
    for src, (rows, cols), to in parts:
        got.append(w.start(src, ext.at[c, rows, cols], w.slot(), to))
    shared = []
    for made, (src, (rows, cols), to) in list(zip(got, parts)):
        made.wait_recv()
        shared.append(w.start(ext.at[c, rows, cols], ext.at[c, rows, cols], w.slot(), sib))
    for made in shared:
        made.wait_recv()
    own.wait()
    w.finish()


def halo_call(obj):
    return pl.pallas_call(
        halo_kernel,
        out_shape=jax.ShapeDtypeStruct((2, EXT, EXT), f32),
        in_specs=[pl.BlockSpec(memory_space=pltpu.VMEM)],
        out_specs=pl.BlockSpec(memory_space=pltpu.VMEM),
        scratch_shapes=[pltpu.SemaphoreType.DMA, pltpu.SemaphoreType.DMA((6,)), pltpu.SemaphoreType.DMA((6,))],
        compiler_params=pltpu.CompilerParams(collective_id=0, has_side_effects=True, vmem_limit_bytes=32 * 2**20),
        name="halo",
    )(obj)


def merge_kernel(channels, frame, sums, obj, probe, out, pout,
                 s, rin, lin, t, fr, fb, fc, acc, wide, hl, hr, tops, bots, up_in, up_edge, dn_in, dn_edge,
                 r0, pa, q, pb, tt, st, pz, send, recv):
    p, z, c, a, b = places()
    nz = N_POS // 2
    half = nz // 2
    up, down = lax.rem(a + N_Y - 1, N_Y), lax.rem(a + 1, N_Y)
    left, right_ = lax.rem(b + N_X - 1, N_X), lax.rem(b + 1, N_X)
    following, previous = lax.rem(p + 1, N_POS), lax.rem(p + N_POS - 1, N_POS)

    def zat(k):
        return lax.rem(z + (k + nz), nz)

    def zdev(k):
        return {"pos": 2 * zat(k) + c}

    sib = {"pos": 2 * z + 1 - c}
    greet([sib] + [zdev(k) for k in range(1, nz)]
          + [{"ty": lax.rem(a + k, N_Y)} for k in range(1, N_Y)]
          + [{"tx": lax.rem(b + k, N_X)} for k in range(1, N_X)]
          + [{"ty": down, "tx": right_}, {"ty": up, "tx": left}]
          + [{"pos": following}, {"pos": previous}]
          + [{"pos": N_POS - 1 - p, "ty": down}, {"pos": N_POS - 1 - p, "ty": up}])
    w = Wires(send, recv)
    up_edge[...] = jnp.zeros_like(up_edge)
    dn_edge[...] = jnp.zeros_like(dn_edge)
    total = frame.shape[0]
    cut = (total + 1) // 2
    parts = (pl.ds(0, cut), pl.ds(cut, total - cut))

    def object_path():
        order = [half]
        for k in range(half - 1, 0, -1):
            order += [k, -k]
        order += [0]
        swaps = {k: w.start(frame.at[:, zat(k), 1 - c], s.at[zat(k)], w.slot(), sib) for k in order}
        yield

        def mine(k):
            swaps[k].wait_recv()
            s[zat(k)] += frame[:, zat(k), c]

        went = {}
        for step in range(half):
            for k in ((half,) if step == 0 else (half - step, step - half)):
                mine(k)
            for part in range(2):
                for way, box in ((1, rin), (-1, lin)):
                    if step == 0 and part != (0 if way == 1 else 1):
                        continue
                    d = zat(way * (half - step))
                    before = went.get((step - 1, way, part))
                    if before is not None:
                        before.wait_recv()
                        s[d, parts[part]] += box[step - 1, parts[part]]
                    went[step, way, part] = w.start(
                        s.at[d, parts[part]], box.at[step, parts[part]], w.slot(), zdev(way))
            yield
        mine(0)
        last = half - 1
        for part in range(2):
            for way, box in ((1, rin), (-1, lin)):
                went[last, way, part].wait_recv()
                s[z, parts[part]] += box[last, parts[part]]
        t[...] = s[z].reshape(channels, 5, 8, EXT)
        f1 = w.start(t.at[:, 0:3, :, TILE:EXT], fr, w.slot(), {"tx": right_})
        f2 = w.start(t.at[:, 3:5, :, 0:TILE], fb, w.slot(), {"ty": down})
        f3 = w.start(t.at[:, 3:5, :, TILE:EXT], fc, w.slot(), {"ty": down, "tx": right_})
        yield
        acc[...] = t[:, 0:3, :, 0:TILE]
        f1.wait_recv()
        acc[:, :, :, 0:N] += fr[...]
        f2.wait_recv()
        acc[:, 0:2] += fb[...]
        f3.wait_recv()
        acc[:, 0:2, :, 0:N] += fc[...]
        share = acc[2] + 1.0
        for ch in range(2):
            wide[ch, :, :, 128:128 + TILE] = obj[ch, :, p] + acc[ch] / share
        h1 = w.start(wide.at[:, :, :, TILE:TILE + 128], hl, w.slot(), {"tx": right_})
        h2 = w.start(wide.at[:, :, :, 128:256], hr, w.slot(), {"tx": left})
        yield
        h1.wait_recv()
        wide[:, :, :, 0:128] = jnp.where(b > 0, hl[...], 0.0)
        h2.wait_recv()
        wide[:, :, :, 128 + TILE:] = jnp.where(b < N_X - 1, hr[...], 0.0)
        tops[...] = jnp.zeros_like(tops)
        bots[...] = jnp.zeros_like(bots)
        for ch in range(2):
            for g in range(3):
                k = 3 * ch + g
                tops[k:k + 1, :] = wide[ch, g, 0:1, :]
                bots[k:k + 1, :] = wide[ch, g, 7:8, :]
        v1 = w.start(bots, up_in, w.slot(), {"pos": following})
        v2 = w.start(tops, dn_in, w.slot(), {"pos": previous})
        k3, k4 = w.slot(), w.slot()

        @pl.when(p == N_POS - 1)
        def _():
            w.copy(bots, up_edge, k3, {"pos": 0, "ty": down}).start()

        @pl.when(p == 0)
        def _():
            w.copy(tops, dn_edge, k4, {"pos": N_POS - 1, "ty": up}).start()

        yield
        v1.wait_recv()
        v2.wait_recv()

        @pl.when(p == 0)
        def _():
            made = w.copy(bots, up_edge, k3, {"pos": 0, "ty": down})
            made.wait_recv()
            w.copy(tops, dn_edge, k4, {"pos": N_POS - 1, "ty": up}).wait_send()

        @pl.when(p == N_POS - 1)
        def _():
            w.copy(tops, dn_edge, k4, {"pos": N_POS - 1, "ty": up}).wait_recv()
            w.copy(bots, up_edge, k3, {"pos": 0, "ty": down}).wait_send()

        sub = lax.broadcasted_iota(jnp.int32, (8, EXT), 0)

        def unit(x, below):
            fx = [pltpu.roll(v, EXT - 1, 1) - v for v in x]
            fy = [n - v for v, n in zip(x, below)]
            power = fx[0] * fx[0] + fy[0] * fy[0] + fx[1] * fx[1] + fy[1] * fy[1]
            mag = jnp.sqrt(jnp.maximum(power, flux_floor))
            return [v / mag for v in fx], [v / mag for v in fy]

        for g in range(3):
            x, above, below = [], [], []
            for ch in range(2):
                k = 3 * ch + g
                v = wide[ch, g]
                if g == 0:
                    edge = jnp.where(a > 0, up_edge[3 * ch + 2:3 * ch + 3, :], 0.0)
                else:
                    edge = up_in[k - 1:k, :]
                first = jnp.where(p == 0, edge, up_in[k:k + 1, :])
                if g == 2:
                    edge = jnp.where(a < N_Y - 1, dn_edge[3 * ch:3 * ch + 1, :], 0.0)
                else:
                    edge = dn_in[k + 1:k + 2, :]
                final = jnp.where(p == N_POS - 1, edge, dn_in[k:k + 1, :])
                x.append(v)
                above.append(jnp.where(sub == 0, first, pltpu.roll(v, 1, 0)))
                below.append(jnp.where(sub == 7, final, pltpu.roll(v, 7, 0)))
            nx, ny = unit(x, below)
            _, my = unit(above, x)
            for ch in range(2):
                div = nx[ch] - pltpu.roll(nx[ch], 1, 1) + ny[ch] - my[ch]
                out[ch, g, p] = (x[ch] + tv_weight * div)[:, 128:128 + TILE]
        went, twin = {}, []

        def twin_send(k):
            q_ = 2 * zat(k) + c
            twin.append(w.start(out.at[:, :, q_], out.at[:, :, q_], w.slot(), sib))

        for step in range(half):
            for way in (1, -1):
                q_ = 2 * zat(-way * step) + c
                for ch in range(2):
                    if step == half - 1 and ch != (0 if way == 1 else 1):
                        continue
                    if step > 0:
                        went[step - 1, way, ch].wait_recv()
                    went[step, way, ch] = w.start(out.at[ch, :, q_], out.at[ch, :, q_], w.slot(), zdev(way))
                if step == half - 1:
                    went[step - 1, way, 1 if way == 1 else 0].wait_recv()
                if step == 0:
                    if way == 1:
                        twin_send(0)
                else:
                    twin_send(-way * step)
            yield
        went[half - 1, 1, 0].wait_recv()
        went[half - 1, -1, 1].wait_recv()
        twin_send(half)
        yield
        for made in twin:
            made.wait_recv()
        yield

    lanes = pl.ds(pl.multiple_of(c * 128, 128), 128)
    others = pl.ds(pl.multiple_of((1 - c) * 128, 128), 128)

    def at_y(k):
        return lax.rem(a + (k + N_Y), N_Y)

    def at_x(k):
        return lax.rem(b + (k + N_X), N_X)

    def probe_path():
        swap = w.start(sums.at[:, :, :, :, :, others], r0, w.slot(), sib)
        yield
        swap.wait_recv()
        r0[...] += sums[:, :, :, :, :, lanes]
        first = []
        for k in range(1, N_Y):
            first.append((0, k, w.start(r0.at[:, at_y(k), :, 0], pa.at[0, k - 1], w.slot(), {"ty": at_y(k)})))
        for k in range(1, N_X):
            first.append((1, k, w.start(r0.at[:, :, at_x(k), 1], pa.at[1, k - 1], w.slot(), {"tx": at_x(k)})))
        yield
        q[0] = r0[:, a, :, 0]
        q[1] = r0[:, :, b, 1]
        for i, k, made in first:
            made.wait_recv()
            q[i] += pa[i, k - 1]
        second = []
        for k in range(1, N_X):
            second.append((0, k, w.start(q.at[0, :, at_x(k)], pb.at[0, k - 1], w.slot(), {"tx": at_x(k)})))
        for k in range(1, N_Y):
            second.append((1, k, w.start(q.at[1, :, at_y(k)], pb.at[1, k - 1], w.slot(), {"ty": at_y(k)})))
        yield
        tt[:, 0] = q[0, :, b]
        tt[:, 1] = q[1, :, a]
        for i, k, made in second:
            made.wait_recv()
            tt[:, i] += pb[i, k - 1]
        st[:, 0] = tt[0:8]
        for k in range(nz):
            st[k, 1] = tt[8]
        third = [w.start(st.at[zat(k)], pz.at[k - 1], w.slot(), zdev(k)) for k in range(1, nz)]
        yield
        whole = st[z]
        for k in range(1, nz):
            third[k - 1].wait_recv()
            whole = whole + pz[k - 1]
        pout[z, a, b, :, :, lanes] = probe[z, a, b, :, :, lanes] + whole[0] / (whole[1] + 1.0)
        spot = pout.at[z, a, b, :, :, lanes]
        fourth = [w.start(spot, spot, w.slot(), zdev(k)) for k in range(1, nz)]
        yield
        for made in fourth:
            made.wait_recv()
        fifth = []
        spot = pout.at[:, a, b, 0, :, lanes]
        for k in range(1, N_X):
            fifth.append(w.start(spot, spot, w.slot(), {"tx": at_x(k)}))
        spot = pout.at[:, a, b, 1, :, lanes]
        for k in range(1, N_Y):
            fifth.append(w.start(spot, spot, w.slot(), {"ty": at_y(k)}))
        yield
        for made in fifth:
            made.wait_recv()
        sixth = []
        spot = pout.at[:, a, :, 0, :, lanes]
        for k in range(1, N_Y):
            sixth.append(w.start(spot, spot, w.slot(), {"ty": at_y(k)}))
        spot = pout.at[:, :, b, 1, :, lanes]
        for k in range(1, N_X):
            sixth.append(w.start(spot, spot, w.slot(), {"tx": at_x(k)}))
        yield
        for made in sixth:
            made.wait_recv()
        spot = pout.at[:, :, :, :, :, lanes]
        last = w.start(spot, spot, w.slot(), sib)
        yield
        last.wait_recv()
        yield

    objects, probes = object_path(), probe_path()
    for turn in MERGE_ORDER:
        next({"o": objects, "p": probes}[turn])
    for path in (objects, probes):
        for _ in path:
            pass
    w.finish()


MERGE_ORDER = "opo" + "po" + "opo" + "pop" + "opopo" + "oo"
MERGE_WIRES = 110


def merge_call(frame, sums, obj, probe):
    channels = frame.shape[0]
    vm = pl.BlockSpec(memory_space=pltpu.VMEM)
    nz = N_POS // 2
    g = 5 * channels
    half = nz // 2

    def v(*shape):
        return pltpu.VMEM(shape, f32)

    out, pout = pl.pallas_call(
        functools.partial(merge_kernel, channels),
        out_shape=(
            jax.ShapeDtypeStruct((2, 3, N_POS, 8, TILE), f32),
            jax.ShapeDtypeStruct((8, N_Y, N_X, 2, 8, N), f32),
        ),
        in_specs=[vm] * 4,
        out_specs=(vm, vm),
        scratch_shapes=[
            v(nz, g, 8, EXT), v(half, g, 8, EXT), v(half, g, 8, EXT), v(channels, 5, 8, EXT),
            v(channels, 3, 8, N), v(channels, 2, 8, TILE), v(channels, 2, 8, N), v(channels, 3, 8, TILE),
            v(2, 3, 8, EXT), v(2, 3, 8, 128), v(2, 3, 8, 128),
            v(8, EXT), v(8, EXT), v(8, EXT), v(8, EXT), v(8, EXT), v(8, EXT),
            v(9, N_Y, N_X, 2, 8, 128), v(2, 3, 9, 4, 8, 128), v(2, 9, 4, 8, 128), v(2, 3, 9, 8, 128),
            v(9, 2, 8, 128), v(8, 2, 2, 8, 128), v(7, 2, 2, 8, 128),
            pltpu.SemaphoreType.DMA((MERGE_WIRES,)), pltpu.SemaphoreType.DMA((MERGE_WIRES,)),
        ],
        compiler_params=pltpu.CompilerParams(collective_id=1, has_side_effects=True, vmem_limit_bytes=56 * 2**20),
        name="merge",
    )(frame.reshape(g, nz, 2, 8, EXT), sums.reshape(9, N_Y, N_X, 2, 8, N),
      obj.reshape(2, 3, N_POS, 8, TILE), probe.reshape(8, N_Y, N_X, 2, 8, N))
    return out.reshape(2, TILE, TILE), pout.reshape(probe.shape)


def body(object_field, probe, amplitudes, live_pixels, offsets):
    base = jnp.stack([lax.axis_index("ty"), lax.axis_index("tx")]).astype(jnp.int32) * TILE
    ext = halo_call(object_field)
    frame, sums = compute_call(offsets - base, ext, probe, amplitudes, live_pixels)
    return merge_call(frame, sums, object_field, probe)


def solution(mesh):
    return jax.shard_map(
        body,
        mesh=mesh,
        in_specs=(
            P(None, "ty", "tx"),
            P(),
            P(("pos", "ty", "tx"), None, None),
            P(),
            P(("pos", "ty", "tx"), None),
        ),
        out_specs=(P(None, "ty", "tx"), P()),
        check_vma=False,
    )
```

```python
import functools, math
import numpy as np, ml_dtypes
import jax, jax.numpy as jnp
from jax import lax
from jax.experimental import pallas as pl
from jax.experimental.pallas import tpu as pltpu
from jax.sharding import PartitionSpec as P

N = 256
H = 128
TILE = 384
EXT = 640
intensity_floor = 0.25
flux_floor = 0.25
tv_weight = 0.1
N_POS, N_Y, N_X = 16, 4, 4
f32, bf16 = jnp.float32, jnp.bfloat16


def tables():
    k = np.arange(H)
    ang = 2.0 * np.pi * ((k[:, None] * k[None, :]) % H) / H
    c, s = np.cos(ang) / 16.0, np.sin(ang) / 16.0
    m = np.block([[c, -s], [s, c]]).astype(np.float32)
    hi = m.astype(ml_dtypes.bfloat16)
    lo = (m - hi.astype(np.float32)).astype(ml_dtypes.bfloat16)
    th = 2.0 * np.pi * k / N
    tw = np.stack([np.cos(th), np.sin(th)]).astype(np.float32)
    turns = np.stack([np.tile(tw[0][:, None], (1, H)), np.tile(tw[1][:, None], (1, H)),
                      np.tile(tw[0], (H, 1)), np.tile(tw[1], (H, 1))])
    perm = np.concatenate([np.arange(0, N, 2), np.arange(1, N, 2)])
    pick = np.zeros((N, N), np.float32)
    pick[np.arange(N), perm] = 1.0
    pick = pick.astype(ml_dtypes.bfloat16)
    return np.stack([hi, lo, hi.T, lo.T, pick, pick.T]), turns


def split(x):
    hi = x.astype(bf16)
    lo = (x - hi.astype(f32)).astype(bf16)
    return hi, lo


def over(hi, lo):
    return jnp.concatenate([hi, hi, lo], 0)


def beside(hi, lo):
    return jnp.concatenate([hi, hi, lo], 1)


def right(x, table):
    hi, lo = split(x)
    return jnp.dot(jnp.concatenate([hi, lo, hi], 1), table, preferred_element_type=f32)


def left(table, x):
    hi, lo = split(x)
    return jnp.dot(table, jnp.concatenate([hi, lo, hi], 0), preferred_element_type=f32)


def split_dot_l(p, x):
    hi, lo = split(x)
    return jnp.dot(p, hi, preferred_element_type=f32) + jnp.dot(p, lo, preferred_element_type=f32)


def split_dot_r(x, p):
    hi, lo = split(x)
    return jnp.dot(hi, p, preferred_element_type=f32) + jnp.dot(lo, p, preferred_element_type=f32)


def shift_up_left(x, srow, scol):
    lane = lax.broadcasted_iota(jnp.int32, (N + 8, 128), 1)
    back = lax.rem(128 - scol, 128)
    turned = [pltpu.roll(x[:, 128 * i:128 * (i + 1)], back, 1) for i in range(3)]
    keep = lane < 128 - scol
    x = jnp.concatenate([jnp.where(keep, turned[i], turned[i + 1]) for i in range(2)], 1)
    x = x.reshape(N // 8 + 1, 8, N)
    x = pltpu.roll(x, lax.rem(8 - srow, 8), 1)
    sub = lax.broadcasted_iota(jnp.int32, (N // 8, 8, N), 1)
    return jnp.where(sub < 8 - srow, x[:-1], x[1:]).reshape(N, N)


def shift_down_right(x, srow, scol):
    x = pltpu.roll(x.reshape(N // 8, 8, N), srow, 1)
    none = jnp.zeros((1, 8, N), f32)
    sub = lax.broadcasted_iota(jnp.int32, (N // 8 + 1, 8, N), 1)
    x = jnp.where(sub >= srow, jnp.concatenate([x, none], 0), jnp.concatenate([none, x], 0))
    x = x.reshape(N + 8, N)
    lane = lax.broadcasted_iota(jnp.int32, (N + 8, 128), 1)
    t = [pltpu.roll(x[:, 128 * i:128 * (i + 1)], scol, 1) for i in range(2)]
    keep = lane >= scol
    return jnp.concatenate([jnp.where(keep, t[0], 0.0), jnp.where(keep, t[1], t[0]), jnp.where(keep, 0.0, t[1])], 1)


STRIDES = ((32, 64), (16, 48), (8, 40), (4, 36), (2, 34), (1, 33))


def bit_of(x, bit):
    return lax.rem(lax.div(x, bit), 2) == 1


def cut_window(ext, c, row, col):
    row8, u = lax.div(row, 8), lax.div(col, 128)
    blocks = [ext[c, :, 128 * i:128 * (i + 1)].reshape(EXT // 8, 8, 128) for i in range(5)]
    out = []
    for o in range(3):
        v = jnp.where(u == 0, blocks[o], jnp.where(u == 1, blocks[o + 1], blocks[o + 2]))
        for bit, size in STRIDES:
            if bit == 32:
                v = jnp.concatenate([jnp.where(bit_of(row8, bit), v[32:80], v[0:48]), v[48:64]], 0)
            else:
                v = jnp.where(bit_of(row8, bit), v[bit:bit + size], v[:size])
        out.append(v.reshape(N + 8, 128))
    return shift_up_left(jnp.concatenate(out, 1), row - 8 * row8, col - 128 * u)


def add_window(frame, c, x, row, col):
    row8, u = lax.div(row, 8), lax.div(col, 128)
    moved = shift_down_right(x, row - 8 * row8, col - 128 * u)
    placed = []
    for o in range(3):
        v = moved[:, 128 * o:128 * (o + 1)].reshape(N // 8 + 1, 8, 128)
        for bit in (1, 2, 4, 8, 16):
            none = jnp.zeros((bit, 8, 128), f32)
            v = jnp.where(bit_of(row8, bit), jnp.concatenate([none, v], 0), jnp.concatenate([v, none], 0))
        none = jnp.zeros((32, 8, 128), f32)
        v = jnp.where(bit_of(row8, 32), jnp.concatenate([none, v[:48]], 0), jnp.concatenate([v, none[:16]], 0))
        placed.append(v)
    none = jnp.zeros((EXT // 8, 8, 128), f32)

    def at(k):
        return placed[k] if 0 <= k < 3 else none

    for o in range(5):
        v = jnp.where(u == 0, at(o), jnp.where(u == 1, at(o - 1), at(o - 2)))
        frame[5 * c:5 * c + 5, :, :, :, 128 * o:128 * (o + 1)] += v.reshape(5, *frame.shape[1:4], 128)


def prepare(live, probe, squares, mask, wparts):
    power = jnp.zeros((N, N), f32)
    for m in range(probe.shape[0]):
        power = power + (probe[m, 0] * probe[m, 0] + probe[m, 1] * probe[m, 1])
    for i in range(3):
        wparts[i] = power.astype(bf16)
        power = power - wparts[i].astype(f32)
    on = (live[...] == 1).astype(bf16)
    on = jnp.dot(squares[4], on, preferred_element_type=f32).astype(bf16)
    mask[...] = jnp.dot(on, squares[5], preferred_element_type=f32)


def visit_positions(slots, offs, ext, probe, amps, squares, turns, frame, sums, patch, far, fac, grad, mask):
    modes = probe.shape[0]
    split_rows = sums.shape[1:]

    @pl.loop(0, slots)
    def _(p):
        row = offs[p, 0] - TILE * lax.axis_index("ty")
        col = offs[p, 1] - TILE * lax.axis_index("tx")
        for c in range(2):
            patch[c] = cut_window(ext, c, row, col)
        pr, pi = patch[0], patch[1]
        sums[2 * modes] += (pr * pr + pi * pi).reshape(split_rows)
        grad[...] = jnp.zeros_like(grad)
        fac[...] = jnp.zeros_like(fac)

        @pl.loop(0, modes, unroll=4)
        def _(m):
            pr, pi = patch[0], patch[1]
            qr, qi = probe[m, 0], probe[m, 1]
            wr = qr * pr - qi * pi
            wi = qr * pi + qi * pr
            ar, ai = wr[:, :H] + wr[:, H:], wi[:, :H] + wi[:, H:]
            br, bi = wr[:, :H] - wr[:, H:], wi[:, :H] - wi[:, H:]
            tc, ts = turns[2, 0:1], turns[3, 0:1]
            br, bi = br * tc + bi * ts, bi * tc - br * ts
            even = right(jnp.concatenate([ar, ai], 1), over(squares[0], squares[1]))
            odd = right(jnp.concatenate([br, bi], 1), over(squares[0], squares[1]))
            total = None
            rc, rs = turns[0], turns[1]
            for h, z in enumerate((even, odd)):
                zr, zi = z[:, :H], z[:, H:]
                ar, ai = zr[:H] + zr[H:], zi[:H] + zi[H:]
                br, bi = zr[:H] - zr[H:], zi[:H] - zi[H:]
                br, bi = br * rc + bi * rs, bi * rc - br * rs
                both = jnp.concatenate([jnp.concatenate([ar, br], 1), jnp.concatenate([ai, bi], 1)], 0)
                out = left(beside(squares[2], squares[3]), both)
                far[m, h] = out
                sq = out * out
                power = sq[:H] + sq[H:]
                fac[h] += power

        amp = split_dot_r(split_dot_l(squares[4], amps[p]), squares[5])
        for h in range(2):
            want = jnp.concatenate([amp[:H, h * H:(h + 1) * H], amp[H:, h * H:(h + 1) * H]], 1)
            lv = jnp.concatenate([mask[:H, h * H:(h + 1) * H], mask[H:, h * H:(h + 1) * H]], 1)
            fac[h] = jnp.where(lv > 0.5, want * lax.rsqrt(jnp.maximum(fac[h], intensity_floor)), 1.0)

        @pl.loop(0, modes, unroll=4)
        def _(m):
            rc, rs = turns[0], turns[1]
            halves = []
            for h in range(2):
                f = far[m, h]
                k = fac[h]
                y = jnp.concatenate([f[:H] * k, f[H:] * k], 0)
                x = left(beside(squares[0], squares[1]), y)
                er, orr = x[:H, :H], x[:H, H:]
                ei, oi = x[H:, :H], x[H:, H:]
                orr, oi = orr * rc - oi * rs, oi * rc + orr * rs
                top = jnp.concatenate([er + orr, ei + oi], 1)
                bottom = jnp.concatenate([er - orr, ei - oi], 1)
                halves.append(right(jnp.concatenate([top, bottom], 0), over(squares[2], squares[3])))
            e, o = halves
            er, ei, orr, oi = e[:, :H], e[:, H:], o[:, :H], o[:, H:]
            tc, ts = turns[2, 0:1], turns[3, 0:1]
            orr, oi = orr * tc - oi * ts, oi * tc + orr * ts
            nr = jnp.concatenate([er + orr, er - orr], 1)
            ni = jnp.concatenate([ei + oi, ei - oi], 1)
            pr, pi = patch[0], patch[1]
            qr, qi = probe[m, 0], probe[m, 1]
            dr = nr - (qr * pr - qi * pi)
            di = ni - (qr * pi + qi * pr)
            grad[0] += qr * dr + qi * di
            grad[1] += qr * di - qi * dr
            sums[2 * m] += (pr * dr + pi * di).reshape(split_rows)
            sums[2 * m + 1] += (pr * di - pi * dr).reshape(split_rows)

        for c in range(2):
            add_window(frame, c, grad[c], row, col)


MESH = pl.DeviceIdType.MESH


class Wires:
    def __init__(self, send, recv):
        self.send, self.recv, self.count, self.started = send, recv, 0, []

    def slot(self):
        self.count += 1
        return self.count - 1

    def copy(self, src, dst, slot, to):
        return pltpu.make_async_remote_copy(
            src_ref=src, dst_ref=dst, send_sem=self.send.at[slot], recv_sem=self.recv.at[slot],
            device_id=to, device_id_type=MESH)

    def start(self, src, dst, slot, to):
        made = self.copy(src, dst, slot, to)
        made.start()
        self.started.append(made)
        return made

    def finish(self):
        for made in self.started:
            made.wait_send()


def greet(partners):
    barrier = pltpu.get_barrier_semaphore()
    for to in partners:
        pl.semaphore_signal(barrier, inc=1, device_id=to, device_id_type=MESH)
    pl.semaphore_wait(barrier, len(partners))


def places():
    p = lax.axis_index("pos")
    return p, p // 2, lax.rem(p, 2), lax.axis_index("ty"), lax.axis_index("tx")


SHARED = 4


def gather_halo(w, offs, obj, ext, table, here, ready):
    p, z, c, a, b = places()
    nz = N_POS // 2
    tile = obj.shape[1]
    up, down = lax.rem(a + N_Y - 1, N_Y), lax.rem(a + 1, N_Y)
    left, right_ = lax.rem(b + N_X - 1, N_X), lax.rem(b + 1, N_X)
    after, before = {"pos": 2 * lax.rem(z + 1, nz) + c}, {"pos": 2 * lax.rem(z + nz - 1, nz) + c}
    sib = {"pos": 2 * z + 1 - c}
    odd = lax.rem(z, 2)
    group = [{"pos": lax.rem(p + k, N_POS)} for k in range(1, N_POS)]
    own = pltpu.make_async_copy(obj, ext.at[:, 0:tile, 0:tile], here)
    own.start()

    def spans(e, k):
        if k == SHARED:
            return pl.ds(256, 128), pl.ds(192, 64)
        return (pl.ds(pl.multiple_of(128 * e + 32 * k, 8), 32), pl.ds(pl.multiple_of(96 * e + 24 * k, 8), 24))

    def lower(rows):
        return pl.ds(pl.multiple_of(tile + rows.start, 8), rows.size)

    def rims(e, k):
        side, below = spans(e, k)
        return ext.at[c, side, tile:tile + N], ext.at[c, lower(below), :]

    came = []
    for k in range(SHARED + 1):
        side, below = spans(odd, k)
        came.append((
            w.start(obj.at[c, side, 0:N], ext.at[c, side, tile:tile + N], w.slot(), {"tx": left}),
            w.start(obj.at[c, below, :], ext.at[c, lower(below), 0:tile], w.slot(), {"ty": up}),
            w.start(obj.at[c, below, 0:N], ext.at[c, lower(below), tile:tile + N], w.slot(), {"ty": up, "tx": left}),
        ))
    lane = lax.broadcasted_iota(jnp.int32, (1, 128), 1)
    row = jnp.zeros((1, 128), jnp.int32)
    for i in range(2 * offs.shape[0]):
        row = jnp.where(lane == i, offs[i // 2, i % 2], row)
    table[0, p] = row
    line = table.at[0, p]
    lines = [w.start(line, line, w.slot(), to) for to in group]
    ready()
    pair, relay = [], []
    for k in range(SHARED + 1):
        for made in came[k]:
            made.wait_recv()
        for spot in rims(odd, k):
            if k < SHARED:
                relay.append(w.start(spot, spot, w.slot(), after if k % 2 == 0 else before))
        for spot in rims(odd, k):
            pair.append(w.start(spot, spot, w.slot(), sib))
        if k == 1:
            for made in lines:
                made.wait_recv()
            for t, to in ((1, {"ty": down}), (2, {"tx": right_}), (3, {"ty": down, "tx": right_})):
                pair.append(w.start(table.at[0], table.at[t], w.slot(), to))
    for k in range(SHARED):
        for i, spot in enumerate(rims(1 - odd, k)):
            relay[2 * k + i].wait_recv()
            pair.append(w.start(spot, spot, w.slot(), sib))
    for made in pair:
        made.wait_recv()
    own.wait()


def step_kernel(offs, obj_far, probe_far, amps_far, live_far, squares_far, turns_far, out, pout,
                ext, table, offs_all, whole_probe, amps, live, squares, turns, patch, far, fac, grad, mask,
                frame, sums, obj, probe, wparts, hot, rows_of, wsum,
                s, rin, lin, t, fr, fb, fc, acc, wide, hl, hr, tops, bots, up_in, up_edge, dn_in, dn_edge,
                r0, pa, q, pb, tt, st, pz, here, send, recv):
    channels = 2
    p, z, c, a, b = places()
    lanes = pl.ds(pl.multiple_of(c * 128, 128), 128)
    others = pl.ds(pl.multiple_of((1 - c) * 128, 128), 128)
    loads = [pltpu.make_async_copy(src, dst, here.at[i]) for i, (src, dst) in enumerate((
        (obj_far.at[:, :, p], obj), (probe_far.at[z, a, b, :, :, lanes], probe),
        (probe_far.reshape(whole_probe.shape), whole_probe), (squares_far, squares), (turns_far, turns),
        (live_far, live), (amps_far, amps)))]
    for load in loads:
        load.start()
    nz = N_POS // 2
    half = nz // 2
    up, down = lax.rem(a + N_Y - 1, N_Y), lax.rem(a + 1, N_Y)
    left, right_ = lax.rem(b + N_X - 1, N_X), lax.rem(b + 1, N_X)
    following, previous = lax.rem(p + 1, N_POS), lax.rem(p + N_POS - 1, N_POS)

    def zat(k):
        return lax.rem(z + (k + nz), nz)

    def zdev(k):
        return {"pos": 2 * zat(k) + c}

    sib = {"pos": 2 * z + 1 - c}
    up_edge[...] = jnp.zeros_like(up_edge)
    dn_edge[...] = jnp.zeros_like(dn_edge)
    greet([{"ty": lax.rem(a + k, N_Y)} for k in range(1, N_Y)]
          + [{"tx": lax.rem(b + k, N_X)} for k in range(1, N_X)]
          + [{"ty": down, "tx": right_}, {"ty": up, "tx": left}]
          + [{"pos": lax.rem(p + k, N_POS)} for k in range(1, N_POS)]
          + [{"pos": N_POS - 1 - p, "ty": down}, {"pos": N_POS - 1 - p, "ty": up}])
    w = Wires(send, recv)

    def ready():
        for ref in (frame, sums, wsum):
            ref[...] = jnp.zeros_like(ref)
        for load in loads[2:]:
            load.wait()
        prepare(live, whole_probe, squares, mask, wparts)

    gather_halo(w, offs, obj_far.reshape(2, TILE, TILE), ext, table, here.at[7], ready)
    known = pltpu.make_async_copy(table, offs_all, here.at[8])
    known.start()
    visit_positions(amps.shape[0], offs, ext, whole_probe, amps, squares, turns, frame, sums,
                    patch, far, fac, grad, mask)
    known.wait()
    spread = lax.broadcasted_iota(jnp.int32, (8, N), 1) - lax.broadcasted_iota(jnp.int32, (8, N), 0)
    lane = lax.broadcasted_iota(jnp.int32, (24, 128), 1)

    def weigh(which):
        @pl.loop(0, 2 * N_POS)
        def _(i):
            row = offs_all[which, lax.div(i, 2), 0, 2 * lax.rem(i, 2)] - TILE * a
            for g in range(3):
                first = (g * N_POS + p) * 8 - row
                hot[pl.ds(pl.multiple_of(24 * i + 8 * g, 8), 8), :] = jnp.where(spread == first, 1.0, 0.0)

        pick = hot[...].astype(bf16)
        rows_of[...] = (jnp.dot(pick, wparts[0], preferred_element_type=f32)
                        + jnp.dot(pick, wparts[1], preferred_element_type=f32)
                        + jnp.dot(pick, wparts[2], preferred_element_type=f32))

        def one(i, carry):
            col = offs_all[which, lax.div(i, 2), 0, 2 * lax.rem(i, 2) + 1] - TILE * b
            col = jnp.clip(col + TILE, 0, 2 * TILE)
            u = lax.div(col, 128)
            s_ = col - 128 * u
            u = u - 3
            x = rows_of[pl.ds(pl.multiple_of(24 * i, 8), 24), :]
            t0, t1 = pltpu.roll(x[:, :128], s_, 1), pltpu.roll(x[:, 128:], s_, 1)
            keep = lane >= s_
            g0, g1, g2 = jnp.where(keep, t0, 0.0), jnp.where(keep, t1, t0), jnp.where(keep, 0.0, t1)
            return tuple(
                carry[o] + jnp.where(u == o, g0, jnp.where(u == o - 1, g1, jnp.where(u == o - 2, g2, 0.0)))
                for o in range(3))

        zero = jnp.zeros((24, 128), f32)
        added = lax.fori_loop(0, 2 * N_POS, one, (zero,) * 3, unroll=4)
        wsum[...] += jnp.concatenate(added, 1)

    total = frame.shape[0]
    cut = (total + 1) // 2
    parts = (pl.ds(0, cut), pl.ds(cut, total - cut))

    def object_path():
        order = [half]
        for k in range(half - 1, 0, -1):
            order += [k, -k]
        order += [0]
        swaps = {k: w.start(frame.at[:, zat(k), 1 - c], s.at[zat(k)], w.slot(), sib) for k in order}
        yield

        def mine(k):
            swaps[k].wait_recv()
            s[zat(k)] += frame[:, zat(k), c]

        went = {}
        for step in range(half):
            for k in ((half,) if step == 0 else (half - step, step - half)):
                mine(k)
            for part in range(2):
                for way, box in ((1, rin), (-1, lin)):
                    if step == 0 and part != (0 if way == 1 else 1):
                        continue
                    d = zat(way * (half - step))
                    before = went.get((step - 1, way, part))
                    if before is not None:
                        before.wait_recv()
                        s[d, parts[part]] += box[step - 1, parts[part]]
                    went[step, way, part] = w.start(
                        s.at[d, parts[part]], box.at[step, parts[part]], w.slot(), zdev(way))
            weigh(step)
            yield
        mine(0)
        last = half - 1
        for part in range(2):
            for way, box in ((1, rin), (-1, lin)):
                went[last, way, part].wait_recv()
                s[z, parts[part]] += box[last, parts[part]]
        t[...] = s[z].reshape(channels, 5, 8, EXT)
        f1 = w.start(t.at[:, 0:3, :, TILE:EXT], fr, w.slot(), {"tx": right_})
        f2 = w.start(t.at[:, 3:5, :, 0:TILE], fb, w.slot(), {"ty": down})
        f3 = w.start(t.at[:, 3:5, :, TILE:EXT], fc, w.slot(), {"ty": down, "tx": right_})
        yield
        acc[...] = t[:, 0:3, :, 0:TILE]
        f1.wait_recv()
        acc[:, :, :, 0:N] += fr[...]
        f2.wait_recv()
        acc[:, 0:2] += fb[...]
        f3.wait_recv()
        acc[:, 0:2, :, 0:N] += fc[...]
        share = wsum[...].reshape(3, 8, TILE) + 1.0
        loads[0].wait()
        for ch in range(2):
            wide[ch, :, :, 128:128 + TILE] = obj[ch] + acc[ch] / share
        h1 = w.start(wide.at[:, :, :, TILE:TILE + 128], hl, w.slot(), {"tx": right_})
        h2 = w.start(wide.at[:, :, :, 128:256], hr, w.slot(), {"tx": left})
        yield
        h1.wait_recv()
        wide[:, :, :, 0:128] = jnp.where(b > 0, hl[...], 0.0)
        h2.wait_recv()
        wide[:, :, :, 128 + TILE:] = jnp.where(b < N_X - 1, hr[...], 0.0)
        tops[...] = jnp.zeros_like(tops)
        bots[...] = jnp.zeros_like(bots)
        for ch in range(2):
            for g in range(3):
                k = 3 * ch + g
                tops[k:k + 1, :] = wide[ch, g, 0:1, :]
                bots[k:k + 1, :] = wide[ch, g, 7:8, :]
        v1 = w.start(bots, up_in, w.slot(), {"pos": following})
        v2 = w.start(tops, dn_in, w.slot(), {"pos": previous})
        k3, k4 = w.slot(), w.slot()

        @pl.when(p == N_POS - 1)
        def _():
            w.copy(bots, up_edge, k3, {"pos": 0, "ty": down}).start()

        @pl.when(p == 0)
        def _():
            w.copy(tops, dn_edge, k4, {"pos": N_POS - 1, "ty": up}).start()

        yield
        v1.wait_recv()
        v2.wait_recv()

        @pl.when(p == 0)
        def _():
            made = w.copy(bots, up_edge, k3, {"pos": 0, "ty": down})
            made.wait_recv()
            w.copy(tops, dn_edge, k4, {"pos": N_POS - 1, "ty": up}).wait_send()

        @pl.when(p == N_POS - 1)
        def _():
            w.copy(tops, dn_edge, k4, {"pos": N_POS - 1, "ty": up}).wait_recv()
            w.copy(bots, up_edge, k3, {"pos": 0, "ty": down}).wait_send()

        sub = lax.broadcasted_iota(jnp.int32, (8, EXT), 0)

        def unit(x, below):
            fx = [pltpu.roll(v, EXT - 1, 1) - v for v in x]
            fy = [n - v for v, n in zip(x, below)]
            power = fx[0] * fx[0] + fy[0] * fy[0] + fx[1] * fx[1] + fy[1] * fy[1]
            mag = jnp.sqrt(jnp.maximum(power, flux_floor))
            return [v / mag for v in fx], [v / mag for v in fy]

        for g in range(3):
            x, above, below = [], [], []
            for ch in range(2):
                k = 3 * ch + g
                v = wide[ch, g]
                if g == 0:
                    edge = jnp.where(a > 0, up_edge[3 * ch + 2:3 * ch + 3, :], 0.0)
                else:
                    edge = up_in[k - 1:k, :]
                first = jnp.where(p == 0, edge, up_in[k:k + 1, :])
                if g == 2:
                    edge = jnp.where(a < N_Y - 1, dn_edge[3 * ch:3 * ch + 1, :], 0.0)
                else:
                    edge = dn_in[k + 1:k + 2, :]
                final = jnp.where(p == N_POS - 1, edge, dn_in[k:k + 1, :])
                x.append(v)
                above.append(jnp.where(sub == 0, first, pltpu.roll(v, 1, 0)))
                below.append(jnp.where(sub == 7, final, pltpu.roll(v, 7, 0)))
            nx, ny = unit(x, below)
            _, my = unit(above, x)
            for ch in range(2):
                div = nx[ch] - pltpu.roll(nx[ch], 1, 1) + ny[ch] - my[ch]
                out[ch, g, p] = (x[ch] + tv_weight * div)[:, 128:128 + TILE]
        went, twin = {}, []

        def twin_send(k):
            q_ = 2 * zat(k) + c
            twin.append(w.start(out.at[:, :, q_], out.at[:, :, q_], w.slot(), sib))

        for step in range(half):
            for way in (1, -1):
                q_ = 2 * zat(-way * step) + c
                for ch in range(2):
                    if step == half - 1 and ch != (0 if way == 1 else 1):
                        continue
                    if step > 0:
                        went[step - 1, way, ch].wait_recv()
                    went[step, way, ch] = w.start(out.at[ch, :, q_], out.at[ch, :, q_], w.slot(), zdev(way))
                if step == half - 1:
                    went[step - 1, way, 1 if way == 1 else 0].wait_recv()
                if step == 0:
                    if way == 1:
                        twin_send(0)
                else:
                    twin_send(-way * step)
            yield
        went[half - 1, 1, 0].wait_recv()
        went[half - 1, -1, 1].wait_recv()
        twin_send(half)
        yield
        for made in twin:
            made.wait_recv()
        yield

    def at_y(k):
        return lax.rem(a + (k + N_Y), N_Y)

    def at_x(k):
        return lax.rem(b + (k + N_X), N_X)

    def probe_path():
        swap = w.start(sums.at[:, :, :, :, :, others], r0, w.slot(), sib)
        yield
        swap.wait_recv()
        r0[...] += sums[:, :, :, :, :, lanes]
        first = []
        for k in range(1, N_Y):
            first.append((0, k, w.start(r0.at[:, at_y(k), :, 0], pa.at[0, k - 1], w.slot(), {"ty": at_y(k)})))
        for k in range(1, N_X):
            first.append((1, k, w.start(r0.at[:, :, at_x(k), 1], pa.at[1, k - 1], w.slot(), {"tx": at_x(k)})))
        yield
        q[0] = r0[:, a, :, 0]
        q[1] = r0[:, :, b, 1]
        for i, k, made in first:
            made.wait_recv()
            q[i] += pa[i, k - 1]
        second = []
        for k in range(1, N_X):
            second.append((0, k, w.start(q.at[0, :, at_x(k)], pb.at[0, k - 1], w.slot(), {"tx": at_x(k)})))
        for k in range(1, N_Y):
            second.append((1, k, w.start(q.at[1, :, at_y(k)], pb.at[1, k - 1], w.slot(), {"ty": at_y(k)})))
        yield
        tt[:, 0] = q[0, :, b]
        tt[:, 1] = q[1, :, a]
        for i, k, made in second:
            made.wait_recv()
            tt[:, i] += pb[i, k - 1]
        st[:, 0] = tt[0:8]
        for k in range(nz):
            st[k, 1] = tt[8]
        third = [w.start(st.at[zat(k)], pz.at[k - 1], w.slot(), zdev(k)) for k in range(1, nz)]
        yield
        whole = st[z]
        for k in range(1, nz):
            third[k - 1].wait_recv()
            whole = whole + pz[k - 1]
        loads[1].wait()
        pout[z, a, b, :, :, lanes] = probe[...] + whole[0] / (whole[1] + 1.0)
        spot = pout.at[z, a, b, :, :, lanes]
        fourth = [w.start(spot, spot, w.slot(), zdev(k)) for k in range(1, nz)]
        yield
        for made in fourth:
            made.wait_recv()
        fifth = []
        spot = pout.at[:, a, b, 0, :, lanes]
        for k in range(1, N_X):
            fifth.append(w.start(spot, spot, w.slot(), {"tx": at_x(k)}))
        spot = pout.at[:, a, b, 1, :, lanes]
        for k in range(1, N_Y):
            fifth.append(w.start(spot, spot, w.slot(), {"ty": at_y(k)}))
        yield
        for made in fifth:
            made.wait_recv()
        sixth = []
        spot = pout.at[:, a, :, 0, :, lanes]
        for k in range(1, N_Y):
            sixth.append(w.start(spot, spot, w.slot(), {"ty": at_y(k)}))
        spot = pout.at[:, :, b, 1, :, lanes]
        for k in range(1, N_X):
            sixth.append(w.start(spot, spot, w.slot(), {"tx": at_x(k)}))
        yield
        for made in sixth:
            made.wait_recv()
        spot = pout.at[:, :, :, :, :, lanes]
        last = w.start(spot, spot, w.slot(), sib)
        yield
        last.wait_recv()
        yield

    objects, probes = object_path(), probe_path()
    for turn in MERGE_ORDER:
        next({"o": objects, "p": probes}[turn])
    for path in (objects, probes):
        for _ in path:
            pass
    w.finish()


MERGE_ORDER = "opo" + "po" + "opo" + "pop" + "opopo" + "oo"
WIRES = 170


def step_call(offs, obj, probe, amps, live):
    channels = 2
    vm = pl.BlockSpec(memory_space=pltpu.VMEM)
    far = pl.BlockSpec(memory_space=pl.ANY)
    nz = N_POS // 2
    g = 5 * channels
    half = nz // 2
    modes = probe.shape[0]
    consts = [jnp.asarray(x) for x in tables()]

    def v(*shape):
        return pltpu.VMEM(shape, f32)

    out, pout = pl.pallas_call(
        step_kernel,
        out_shape=(
            jax.ShapeDtypeStruct((2, 3, N_POS, 8, TILE), f32),
            jax.ShapeDtypeStruct((8, N_Y, N_X, 2, 8, N), f32),
        ),
        in_specs=[pl.BlockSpec(memory_space=pltpu.SMEM)] + [far] * 6,
        out_specs=(vm, vm),
        scratch_shapes=[
            v(2, EXT, EXT), pltpu.VMEM((4, N_POS, 1, 128), jnp.int32), pltpu.SMEM((4, N_POS, 1, 128), jnp.int32),
            v(*probe.shape), v(*amps.shape), pltpu.VMEM((N, N), jnp.int32), pltpu.VMEM((6, N, N), bf16), v(4, H, H),
            v(2, N, N), v(modes, 2, N, N), v(2, H, N), v(2, N, N), v(N, N),
            v(g, nz, 2, 8, EXT), v(9, N_Y, N_X, 2, 8, N),
            v(2, 3, 8, TILE), v(2, 8, 128), pltpu.VMEM((3, N, N), bf16),
            v(48 * N_POS, N), v(48 * N_POS, N), v(24, TILE),
            v(nz, g, 8, EXT), v(half, g, 8, EXT), v(half, g, 8, EXT), v(channels, 5, 8, EXT),
            v(channels, 3, 8, N), v(channels, 2, 8, TILE), v(channels, 2, 8, N), v(channels, 3, 8, TILE),
            v(2, 3, 8, EXT), v(2, 3, 8, 128), v(2, 3, 8, 128),
            v(8, EXT), v(8, EXT), v(8, EXT), v(8, EXT), v(8, EXT), v(8, EXT),
            v(9, N_Y, N_X, 2, 8, 128), v(2, 3, 9, 4, 8, 128), v(2, 9, 4, 8, 128), v(2, 3, 9, 8, 128),
            v(9, 2, 8, 128), v(8, 2, 2, 8, 128), v(7, 2, 2, 8, 128),
            pltpu.SemaphoreType.DMA((9,)), pltpu.SemaphoreType.DMA((WIRES,)), pltpu.SemaphoreType.DMA((WIRES,)),
        ],
        compiler_params=pltpu.CompilerParams(collective_id=0, has_side_effects=True, vmem_limit_bytes=60 * 2**20),
        name="step",
    )(offs, obj.reshape(2, 3, N_POS, 8, TILE), probe.reshape(8, N_Y, N_X, 2, 8, N), amps, live, *consts)
    return out.reshape(2, TILE, TILE), pout.reshape(probe.shape)


def body(object_field, probe, amplitudes, live_pixels, offsets):
    return step_call(offsets, object_field, probe, amplitudes, live_pixels)


def solution(mesh):
    return jax.shard_map(
        body,
        mesh=mesh,
        in_specs=(
            P(None, "ty", "tx"),
            P(),
            P(("pos", "ty", "tx"), None, None),
            P(),
            P(("pos", "ty", "tx"), None),
        ),
        out_specs=(P(None, "ty", "tx"), P()),
        check_vma=False,
    )
```

```python
import functools, math
import numpy as np, ml_dtypes
import jax, jax.numpy as jnp
from jax import lax
from jax.experimental import pallas as pl
from jax.experimental.pallas import tpu as pltpu
from jax.sharding import PartitionSpec as P

N = 256
H = 128
TILE = 384
EXT = 640
intensity_floor = 0.25
flux_floor = 0.25
tv_weight = 0.1
N_POS, N_Y, N_X = 16, 4, 4
f32, bf16 = jnp.float32, jnp.bfloat16


def tables():
    k = np.arange(H)
    ang = 2.0 * np.pi * ((k[:, None] * k[None, :]) % H) / H
    c, s = np.cos(ang) / 16.0, np.sin(ang) / 16.0
    m = np.block([[c, -s], [s, c]]).astype(np.float32)
    hi = m.astype(ml_dtypes.bfloat16)
    lo = (m - hi.astype(np.float32)).astype(ml_dtypes.bfloat16)
    th = 2.0 * np.pi * k / N
    tw = np.stack([np.cos(th), np.sin(th)]).astype(np.float32)
    turns = np.stack([np.tile(tw[0][:, None], (1, H)), np.tile(tw[1][:, None], (1, H)),
                      np.tile(tw[0], (H, 1)), np.tile(tw[1], (H, 1))])
    perm = np.concatenate([np.arange(0, N, 2), np.arange(1, N, 2)])
    pick = np.zeros((N, N), np.float32)
    pick[np.arange(N), perm] = 1.0
    pick = pick.astype(ml_dtypes.bfloat16)
    return np.stack([hi, lo, hi.T, lo.T, pick, pick.T]), turns


def split(x):
    hi = x.astype(bf16)
    lo = (x - hi.astype(f32)).astype(bf16)
    return hi, lo


def over(hi, lo):
    return jnp.concatenate([hi, hi, lo], 0)


def beside(hi, lo):
    return jnp.concatenate([hi, hi, lo], 1)


def right(x, table):
    hi, lo = split(x)
    return jnp.dot(jnp.concatenate([hi, lo, hi], 1), table, preferred_element_type=f32)


def left(table, x):
    hi, lo = split(x)
    return jnp.dot(table, jnp.concatenate([hi, lo, hi], 0), preferred_element_type=f32)


def split_dot_l(p, x):
    hi, lo = split(x)
    return jnp.dot(p, hi, preferred_element_type=f32) + jnp.dot(p, lo, preferred_element_type=f32)


def split_dot_r(x, p):
    hi, lo = split(x)
    return jnp.dot(hi, p, preferred_element_type=f32) + jnp.dot(lo, p, preferred_element_type=f32)


def shift_up_left(x, srow, scol):
    lane = lax.broadcasted_iota(jnp.int32, (N + 8, 128), 1)
    back = lax.rem(128 - scol, 128)
    turned = [pltpu.roll(x[:, 128 * i:128 * (i + 1)], back, 1) for i in range(3)]
    keep = lane < 128 - scol
    x = jnp.concatenate([jnp.where(keep, turned[i], turned[i + 1]) for i in range(2)], 1)
    x = x.reshape(N // 8 + 1, 8, N)
    x = pltpu.roll(x, lax.rem(8 - srow, 8), 1)
    sub = lax.broadcasted_iota(jnp.int32, (N // 8, 8, N), 1)
    return jnp.where(sub < 8 - srow, x[:-1], x[1:]).reshape(N, N)


def shift_down_right(x, srow, scol):
    x = pltpu.roll(x.reshape(N // 8, 8, N), srow, 1)
    none = jnp.zeros((1, 8, N), f32)
    sub = lax.broadcasted_iota(jnp.int32, (N // 8 + 1, 8, N), 1)
    x = jnp.where(sub >= srow, jnp.concatenate([x, none], 0), jnp.concatenate([none, x], 0))
    x = x.reshape(N + 8, N)
    lane = lax.broadcasted_iota(jnp.int32, (N + 8, 128), 1)
    t = [pltpu.roll(x[:, 128 * i:128 * (i + 1)], scol, 1) for i in range(2)]
    keep = lane >= scol
    return jnp.concatenate([jnp.where(keep, t[0], 0.0), jnp.where(keep, t[1], t[0]), jnp.where(keep, 0.0, t[1])], 1)


STRIDES = ((32, 64), (16, 48), (8, 40), (4, 36), (2, 34), (1, 33))


def bit_of(x, bit):
    return lax.rem(lax.div(x, bit), 2) == 1


def cut_window(ext, c, row, col):
    row8, u = lax.div(row, 8), lax.div(col, 128)
    blocks = [ext[c, :, 128 * i:128 * (i + 1)].reshape(EXT // 8, 8, 128) for i in range(5)]
    out = []
    for o in range(3):
        v = jnp.where(u == 0, blocks[o], jnp.where(u == 1, blocks[o + 1], blocks[o + 2]))
        for bit, size in STRIDES:
            if bit == 32:
                v = jnp.concatenate([jnp.where(bit_of(row8, bit), v[32:80], v[0:48]), v[48:64]], 0)
            else:
                v = jnp.where(bit_of(row8, bit), v[bit:bit + size], v[:size])
        out.append(v.reshape(N + 8, 128))
    return shift_up_left(jnp.concatenate(out, 1), row - 8 * row8, col - 128 * u)


def add_window(frame, c, x, row, col):
    row8, u = lax.div(row, 8), lax.div(col, 128)
    moved = shift_down_right(x, row - 8 * row8, col - 128 * u)
    placed = []
    for o in range(3):
        v = moved[:, 128 * o:128 * (o + 1)].reshape(N // 8 + 1, 8, 128)
        for bit in (1, 2, 4, 8, 16):
            none = jnp.zeros((bit, 8, 128), f32)
            v = jnp.where(bit_of(row8, bit), jnp.concatenate([none, v], 0), jnp.concatenate([v, none], 0))
        none = jnp.zeros((32, 8, 128), f32)
        v = jnp.where(bit_of(row8, 32), jnp.concatenate([none, v[:48]], 0), jnp.concatenate([v, none[:16]], 0))
        placed.append(v)
    none = jnp.zeros((EXT // 8, 8, 128), f32)

    def at(k):
        return placed[k] if 0 <= k < 3 else none

    for o in range(5):
        v = jnp.where(u == 0, at(o), jnp.where(u == 1, at(o - 1), at(o - 2)))
        frame[5 * c:5 * c + 5, :, :, :, 128 * o:128 * (o + 1)] += v.reshape(5, *frame.shape[1:4], 128)


def prepare(live, probe, squares, mask, wparts):
    power = jnp.zeros((N, N), f32)
    for m in range(probe.shape[0]):
        power = power + (probe[m, 0] * probe[m, 0] + probe[m, 1] * probe[m, 1])
    for i in range(3):
        wparts[i] = power.astype(bf16)
        power = power - wparts[i].astype(f32)
    on = (live[...] == 1).astype(bf16)
    on = jnp.dot(squares[4], on, preferred_element_type=f32).astype(bf16)
    mask[...] = jnp.dot(on, squares[5], preferred_element_type=f32)


def visit_positions(slots, offs, ext, probe, amps, squares, turns, frame, sums, patch, far, fac, grad, mask, hand_over):
    modes = probe.shape[0]
    split_rows = sums.shape[1:]

    @pl.loop(0, slots)
    def _(p):
        row = offs[p, 0] - TILE * lax.axis_index("ty")
        col = offs[p, 1] - TILE * lax.axis_index("tx")
        for c in range(2):
            patch[c] = cut_window(ext, c, row, col)
        pr, pi = patch[0], patch[1]
        sums[2 * modes] += (pr * pr + pi * pi).reshape(split_rows)

        @pl.when(p == slots - 1)
        def _():
            hand_over(modes)

        grad[...] = jnp.zeros_like(grad)
        fac[...] = jnp.zeros_like(fac)

        @pl.loop(0, modes, unroll=4)
        def _(m):
            pr, pi = patch[0], patch[1]
            qr, qi = probe[m, 0], probe[m, 1]
            wr = qr * pr - qi * pi
            wi = qr * pi + qi * pr
            ar, ai = wr[:, :H] + wr[:, H:], wi[:, :H] + wi[:, H:]
            br, bi = wr[:, :H] - wr[:, H:], wi[:, :H] - wi[:, H:]
            tc, ts = turns[2, 0:1], turns[3, 0:1]
            br, bi = br * tc + bi * ts, bi * tc - br * ts
            even = right(jnp.concatenate([ar, ai], 1), over(squares[0], squares[1]))
            odd = right(jnp.concatenate([br, bi], 1), over(squares[0], squares[1]))
            total = None
            rc, rs = turns[0], turns[1]
            for h, z in enumerate((even, odd)):
                zr, zi = z[:, :H], z[:, H:]
                ar, ai = zr[:H] + zr[H:], zi[:H] + zi[H:]
                br, bi = zr[:H] - zr[H:], zi[:H] - zi[H:]
                br, bi = br * rc + bi * rs, bi * rc - br * rs
                both = jnp.concatenate([jnp.concatenate([ar, br], 1), jnp.concatenate([ai, bi], 1)], 0)
                out = left(beside(squares[2], squares[3]), both)
                far[m, h] = out
                sq = out * out
                power = sq[:H] + sq[H:]
                fac[h] += power

        amp = split_dot_r(split_dot_l(squares[4], amps[p]), squares[5])
        for h in range(2):
            want = jnp.concatenate([amp[:H, h * H:(h + 1) * H], amp[H:, h * H:(h + 1) * H]], 1)
            lv = jnp.concatenate([mask[:H, h * H:(h + 1) * H], mask[H:, h * H:(h + 1) * H]], 1)
            fac[h] = jnp.where(lv > 0.5, want * lax.rsqrt(jnp.maximum(fac[h], intensity_floor)), 1.0)

        for m in range(modes):
            rc, rs = turns[0], turns[1]
            halves = []
            for h in range(2):
                f = far[m, h]
                k = fac[h]
                y = jnp.concatenate([f[:H] * k, f[H:] * k], 0)
                x = left(beside(squares[0], squares[1]), y)
                er, orr = x[:H, :H], x[:H, H:]
                ei, oi = x[H:, :H], x[H:, H:]
                orr, oi = orr * rc - oi * rs, oi * rc + orr * rs
                top = jnp.concatenate([er + orr, ei + oi], 1)
                bottom = jnp.concatenate([er - orr, ei - oi], 1)
                halves.append(right(jnp.concatenate([top, bottom], 0), over(squares[2], squares[3])))
            e, o = halves
            er, ei, orr, oi = e[:, :H], e[:, H:], o[:, :H], o[:, H:]
            tc, ts = turns[2, 0:1], turns[3, 0:1]
            orr, oi = orr * tc - oi * ts, oi * tc + orr * ts
            nr = jnp.concatenate([er + orr, er - orr], 1)
            ni = jnp.concatenate([ei + oi, ei - oi], 1)
            pr, pi = patch[0], patch[1]
            qr, qi = probe[m, 0], probe[m, 1]
            dr = nr - (qr * pr - qi * pi)
            di = ni - (qr * pi + qi * pr)
            grad[0] += qr * dr + qi * di
            grad[1] += qr * di - qi * dr
            sums[2 * m] += (pr * dr + pi * di).reshape(split_rows)
            sums[2 * m + 1] += (pr * di - pi * dr).reshape(split_rows)

            @pl.when(p == slots - 1)
            def _():
                hand_over(m)

        for c in range(2):
            add_window(frame, c, grad[c], row, col)


MESH = pl.DeviceIdType.MESH


class Wires:
    def __init__(self, send, recv):
        self.send, self.recv, self.count, self.started = send, recv, 0, []

    def slot(self):
        self.count += 1
        return self.count - 1

    def copy(self, src, dst, slot, to):
        return pltpu.make_async_remote_copy(
            src_ref=src, dst_ref=dst, send_sem=self.send.at[slot], recv_sem=self.recv.at[slot],
            device_id=to, device_id_type=MESH)

    def start(self, src, dst, slot, to):
        made = self.copy(src, dst, slot, to)
        made.start()
        self.started.append(made)
        return made

    def finish(self):
        for made in self.started:
            made.wait_send()


def greet(partners):
    barrier = pltpu.get_barrier_semaphore()
    for to in partners:
        pl.semaphore_signal(barrier, inc=1, device_id=to, device_id_type=MESH)
    pl.semaphore_wait(barrier, len(partners))


def places():
    p = lax.axis_index("pos")
    return p, p // 2, lax.rem(p, 2), lax.axis_index("ty"), lax.axis_index("tx")


SHARED = 4


def gather_halo(w, offs, obj, ext, table, here, ready):
    p, z, c, a, b = places()
    nz = N_POS // 2
    tile = obj.shape[1]
    up, down = lax.rem(a + N_Y - 1, N_Y), lax.rem(a + 1, N_Y)
    left, right_ = lax.rem(b + N_X - 1, N_X), lax.rem(b + 1, N_X)
    after, before = {"pos": 2 * lax.rem(z + 1, nz) + c}, {"pos": 2 * lax.rem(z + nz - 1, nz) + c}
    sib = {"pos": 2 * z + 1 - c}
    odd = lax.rem(z, 2)
    group = [{"pos": lax.rem(p + k, N_POS)} for k in range(1, N_POS)]
    own = pltpu.make_async_copy(obj, ext.at[:, 0:tile, 0:tile], here)
    own.start()

    def spans(e, k):
        if k == SHARED:
            return pl.ds(256, 128), pl.ds(192, 64)
        return (pl.ds(pl.multiple_of(128 * e + 32 * k, 8), 32), pl.ds(pl.multiple_of(96 * e + 24 * k, 8), 24))

    def lower(rows):
        return pl.ds(pl.multiple_of(tile + rows.start, 8), rows.size)

    def rims(e, k):
        side, below = spans(e, k)
        return ext.at[c, side, tile:tile + N], ext.at[c, lower(below), :]

    came = []

    def push(k):
        side, below = spans(odd, k)
        came.append((
            w.start(obj.at[c, side, 0:N], ext.at[c, side, tile:tile + N], w.slot(), {"tx": left}),
            w.start(obj.at[c, below, :], ext.at[c, lower(below), 0:tile], w.slot(), {"ty": up}),
            w.start(obj.at[c, below, 0:N], ext.at[c, lower(below), tile:tile + N], w.slot(), {"ty": up, "tx": left}),
        ))

    push(0)
    for k in range(1, SHARED):
        push(k)
    lane = lax.broadcasted_iota(jnp.int32, (1, 128), 1)
    row = jnp.zeros((1, 128), jnp.int32)
    for i in range(2 * offs.shape[0]):
        row = jnp.where(lane == i, offs[i // 2, i % 2], row)
    table[0, p] = row
    line = table.at[0, p]
    lines = [w.start(line, line, w.slot(), to) for to in group]
    ready()
    pair, relay = [], []
    for k in range(SHARED + 1):
        for made in came[k]:
            made.wait_recv()
        if k == 1:
            push(SHARED)
        for spot in rims(odd, k):
            if k < SHARED:
                relay.append(w.start(spot, spot, w.slot(), after if k % 2 == 0 else before))
        for spot in rims(odd, k):
            pair.append(w.start(spot, spot, w.slot(), sib))
        if k == 1:
            for made in lines:
                made.wait_recv()
            for t, to in ((1, {"ty": down}), (2, {"tx": right_}), (3, {"ty": down, "tx": right_})):
                pair.append(w.start(table.at[0], table.at[t], w.slot(), to))
    for k in range(SHARED):
        for i, spot in enumerate(rims(1 - odd, k)):
            relay[2 * k + i].wait_recv()
            pair.append(w.start(spot, spot, w.slot(), sib))
    for made in pair:
        made.wait_recv()
    own.wait()


def step_kernel(offs, obj_far, probe_far, amps_far, live_far, squares_far, turns_far, out, pout,
                ext, table, offs_all, whole_probe, amps, live, squares, turns, patch, far, fac, grad, mask,
                frame, sums, obj, probe, wparts, hot, rows_of, wsum,
                s, rin, lin, t, fr, fb, fc, acc, wide, hl, hr, tops, bots, up_in, up_edge, dn_in, dn_edge,
                r0, pa, q, pb, tt, st, pz, here, send, recv):
    channels = 2
    p, z, c, a, b = places()
    lanes = pl.ds(pl.multiple_of(c * 128, 128), 128)
    others = pl.ds(pl.multiple_of((1 - c) * 128, 128), 128)
    loads = [pltpu.make_async_copy(src, dst, here.at[i]) for i, (src, dst) in enumerate((
        (obj_far.at[:, :, p], obj), (probe_far.at[z, a, b, :, :, lanes], probe),
        (probe_far.reshape(whole_probe.shape), whole_probe), (squares_far, squares), (turns_far, turns),
        (live_far, live), (amps_far, amps)))]
    for load in loads:
        load.start()
    nz = N_POS // 2
    half = nz // 2
    up, down = lax.rem(a + N_Y - 1, N_Y), lax.rem(a + 1, N_Y)
    left, right_ = lax.rem(b + N_X - 1, N_X), lax.rem(b + 1, N_X)
    following, previous = lax.rem(p + 1, N_POS), lax.rem(p + N_POS - 1, N_POS)

    def zat(k):
        return lax.rem(z + (k + nz), nz)

    def zdev(k):
        return {"pos": 2 * zat(k) + c}

    sib = {"pos": 2 * z + 1 - c}
    for ref in (tops, bots, up_in, up_edge, dn_in, dn_edge):
        ref[...] = jnp.zeros_like(ref)
    greet([{"ty": lax.rem(a + k, N_Y)} for k in range(1, N_Y)]
          + [{"tx": lax.rem(b + k, N_X)} for k in range(1, N_X)]
          + [{"ty": down, "tx": right_}, {"ty": up, "tx": left}]
          + [{"pos": lax.rem(p + k, N_POS)} for k in range(1, N_POS)]
          + [{"pos": N_POS - 1 - p, "ty": down}, {"pos": N_POS - 1 - p, "ty": up}]
          + [{"pos": N_POS - 1 - p, "ty": down, "tx": left}, {"pos": N_POS - 1 - p, "ty": up, "tx": right_}]
          + [{"pos": following, "tx": left}, {"pos": previous, "tx": right_}])
    w = Wires(send, recv)

    def ready():
        for ref in (frame, sums, wsum):
            ref[...] = jnp.zeros_like(ref)
        for load in loads[2:]:
            load.wait()
        prepare(live, whole_probe, squares, mask, wparts)

    gather_halo(w, offs, obj_far.reshape(2, TILE, TILE), ext, table, here.at[7], ready)
    swap_slots = [w.slot() for _ in range(whole_probe.shape[0] + 1)]

    def swap(m):
        two = pl.ds(2 * m, 2 if m < whole_probe.shape[0] else 1)
        return w.copy(sums.at[two, :, :, :, :, others], r0.at[two], swap_slots[m], sib)

    known = pltpu.make_async_copy(table, offs_all, here.at[8])
    known.start()
    visit_positions(amps.shape[0], offs, ext, whole_probe, amps, squares, turns, frame, sums,
                    patch, far, fac, grad, mask, lambda m: swap(m).start())
    known.wait()
    spread = lax.broadcasted_iota(jnp.int32, (8, N), 1) - lax.broadcasted_iota(jnp.int32, (8, N), 0)
    lane = lax.broadcasted_iota(jnp.int32, (24, 128), 1)

    def weigh(which):
        @pl.loop(0, 2 * N_POS)
        def _(i):
            row = offs_all[which, lax.div(i, 2), 0, 2 * lax.rem(i, 2)] - TILE * a
            for g in range(3):
                first = (g * N_POS + p) * 8 - row
                hot[pl.ds(pl.multiple_of(24 * i + 8 * g, 8), 8), :] = jnp.where(spread == first, 1.0, 0.0)

        pick = hot[...].astype(bf16)
        rows_of[...] = (jnp.dot(pick, wparts[0], preferred_element_type=f32)
                        + jnp.dot(pick, wparts[1], preferred_element_type=f32)
                        + jnp.dot(pick, wparts[2], preferred_element_type=f32))

        def one(i, carry):
            col = offs_all[which, lax.div(i, 2), 0, 2 * lax.rem(i, 2) + 1] - TILE * b
            col = jnp.clip(col + TILE, 0, 2 * TILE)
            u = lax.div(col, 128)
            s_ = col - 128 * u
            u = u - 3
            x = rows_of[pl.ds(pl.multiple_of(24 * i, 8), 24), :]
            t0, t1 = pltpu.roll(x[:, :128], s_, 1), pltpu.roll(x[:, 128:], s_, 1)
            keep = lane >= s_
            g0, g1, g2 = jnp.where(keep, t0, 0.0), jnp.where(keep, t1, t0), jnp.where(keep, 0.0, t1)
            return tuple(
                carry[o] + jnp.where(u == o, g0, jnp.where(u == o - 1, g1, jnp.where(u == o - 2, g2, 0.0)))
                for o in range(3))

        zero = jnp.zeros((24, 128), f32)
        added = lax.fori_loop(0, 2 * N_POS, one, (zero,) * 3, unroll=4)
        wsum[...] += jnp.concatenate(added, 1)

    total = frame.shape[0]
    cut = (total + 1) // 2
    parts = (pl.ds(0, cut), pl.ds(cut, total - cut))

    def object_path():
        order = [half]
        for k in range(half - 1, 0, -1):
            order += [k, -k]
        order += [0]
        swaps = {}

        def swap_more(count):
            for k in order[len(swaps):len(swaps) + count]:
                swaps[k] = w.start(frame.at[:, zat(k), 1 - c], s.at[zat(k)], w.slot(), sib)

        swap_more(3)
        yield

        def mine(k):
            swaps[k].wait_recv()
            s[zat(k)] += frame[:, zat(k), c]

        went = {}
        for step in range(half):
            for k in ((half,) if step == 0 else (half - step, step - half)):
                mine(k)
            for part in range(2):
                for way, box in ((1, rin), (-1, lin)):
                    if step == 0 and part != (0 if way == 1 else 1):
                        continue
                    d = zat(way * (half - step))
                    before = went.get((step - 1, way, part))
                    if before is not None:
                        before.wait_recv()
                        s[d, parts[part]] += box[step - 1, parts[part]]
                    went[step, way, part] = w.start(
                        s.at[d, parts[part]], box.at[step, parts[part]], w.slot(), zdev(way))
            swap_more(3)
            weigh(step)
            yield
        mine(0)
        last = half - 1
        for part in range(2):
            for way, box in ((1, rin), (-1, lin)):
                went[last, way, part].wait_recv()
                s[z, parts[part]] += box[last, parts[part]]
        t[...] = s[z].reshape(channels, 5, 8, EXT)
        f1 = w.start(t.at[:, 0:3, :, TILE:EXT], fr, w.slot(), {"tx": right_})
        f2 = w.start(t.at[:, 3:5, :, 0:TILE], fb, w.slot(), {"ty": down})
        f3 = w.start(t.at[:, 3:5, :, TILE:EXT], fc, w.slot(), {"ty": down, "tx": right_})
        yield
        acc[...] = t[:, 0:3, :, 0:TILE]
        f1.wait_recv()
        acc[:, :, :, 0:N] += fr[...]
        f2.wait_recv()
        acc[:, 0:2] += fb[...]
        f3.wait_recv()
        acc[:, 0:2, :, 0:N] += fc[...]
        share = wsum[...].reshape(3, 8, TILE) + 1.0
        loads[0].wait()
        for ch in range(2):
            wide[ch, :, :, 128:128 + TILE] = obj[ch] + acc[ch] / share
        h1 = w.start(wide.at[:, :, :, TILE:TILE + 128], hl, w.slot(), {"tx": right_})
        h2 = w.start(wide.at[:, :, :, 128:256], hr, w.slot(), {"tx": left})
        for ch in range(2):
            for g in range(3):
                k = 3 * ch + g
                tops[k:k + 1, :] = wide[ch, g, 0:1, 128:128 + TILE]
                bots[k:k + 1, :] = wide[ch, g, 7:8, 128:128 + TILE]
        inner, first, final = pl.ds(128, TILE), pl.ds(0, 128), pl.ds(128 + TILE, 128)
        rows_sent = [
            w.start(bots, up_in.at[:, inner], w.slot(), {"pos": following}),
            w.start(tops, dn_in.at[:, inner], w.slot(), {"pos": previous}),
            w.start(bots.at[:, 0:128], up_in.at[:, final], w.slot(), {"pos": following, "tx": left}),
            w.start(tops.at[:, TILE - 128:TILE], dn_in.at[:, first], w.slot(), {"pos": previous, "tx": right_}),
        ]
        k3 = [w.slot(), w.slot()]
        k4 = [w.slot(), w.slot()]

        def last_down():
            return [w.copy(bots, up_edge.at[:, inner], k3[0], {"pos": 0, "ty": down}),
                    w.copy(bots.at[:, 0:128], up_edge.at[:, final], k3[1], {"pos": 0, "ty": down, "tx": left})]

        def first_up():
            return [w.copy(tops, dn_edge.at[:, inner], k4[0], {"pos": N_POS - 1, "ty": up}),
                    w.copy(tops.at[:, TILE - 128:TILE], dn_edge.at[:, first], k4[1],
                           {"pos": N_POS - 1, "ty": up, "tx": right_})]

        @pl.when(p == N_POS - 1)
        def _():
            for made in last_down():
                made.start()

        @pl.when(p == 0)
        def _():
            for made in first_up():
                made.start()

        yield
        h1.wait_recv()
        wide[:, :, :, 0:128] = jnp.where(b > 0, hl[...], 0.0)
        h2.wait_recv()
        wide[:, :, :, 128 + TILE:] = jnp.where(b < N_X - 1, hr[...], 0.0)
        for made in rows_sent:
            made.wait_recv()

        @pl.when(p == 0)
        def _():
            for made in last_down():
                made.wait_recv()
            for made in first_up():
                made.wait_send()

        @pl.when(p == N_POS - 1)
        def _():
            for made in first_up():
                made.wait_recv()
            for made in last_down():
                made.wait_send()

        in_left = lax.broadcasted_iota(jnp.int32, (1, EXT), 1) >= jnp.where(b > 0, 0, 128)
        in_right = lax.broadcasted_iota(jnp.int32, (1, EXT), 1) < jnp.where(b < N_X - 1, EXT, 128 + TILE)
        sub = lax.broadcasted_iota(jnp.int32, (8, EXT), 0)

        def unit(x, below):
            fx = [pltpu.roll(v, EXT - 1, 1) - v for v in x]
            fy = [n - v for v, n in zip(x, below)]
            power = fx[0] * fx[0] + fy[0] * fy[0] + fx[1] * fx[1] + fy[1] * fy[1]
            mag = jnp.sqrt(jnp.maximum(power, flux_floor))
            return [v / mag for v in fx], [v / mag for v in fy]

        for g in range(3):
            x, above, below = [], [], []
            for ch in range(2):
                k = 3 * ch + g
                v = wide[ch, g]
                if g == 0:
                    edge = jnp.where(a > 0, up_edge[3 * ch + 2:3 * ch + 3, :], 0.0)
                else:
                    edge = up_in[k - 1:k, :]
                first = jnp.where(in_right, jnp.where(p == 0, edge, up_in[k:k + 1, :]), 0.0)
                if g == 2:
                    edge = jnp.where(a < N_Y - 1, dn_edge[3 * ch:3 * ch + 1, :], 0.0)
                else:
                    edge = dn_in[k + 1:k + 2, :]
                final = jnp.where(in_left, jnp.where(p == N_POS - 1, edge, dn_in[k:k + 1, :]), 0.0)
                x.append(v)
                above.append(jnp.where(sub == 0, first, pltpu.roll(v, 1, 0)))
                below.append(jnp.where(sub == 7, final, pltpu.roll(v, 7, 0)))
            nx, ny = unit(x, below)
            _, my = unit(above, x)
            for ch in range(2):
                div = nx[ch] - pltpu.roll(nx[ch], 1, 1) + ny[ch] - my[ch]
                out[ch, g, p] = (x[ch] + tv_weight * div)[:, 128:128 + TILE]
        went, twin = {}, []

        def twin_send(k):
            q_ = 2 * zat(k) + c
            twin.append(w.start(out.at[:, :, q_], out.at[:, :, q_], w.slot(), sib))

        for step in range(half):
            for way in (1, -1):
                q_ = 2 * zat(-way * step) + c
                for ch in range(2):
                    if step == half - 1 and ch != (0 if way == 1 else 1):
                        continue
                    if step > 0:
                        went[step - 1, way, ch].wait_recv()
                    went[step, way, ch] = w.start(out.at[ch, :, q_], out.at[ch, :, q_], w.slot(), zdev(way))
                if step == half - 1:
                    went[step - 1, way, 1 if way == 1 else 0].wait_recv()
                if step == 0:
                    if way == 1:
                        twin_send(0)
                else:
                    twin_send(-way * step)
            yield
        went[half - 1, 1, 0].wait_recv()
        went[half - 1, -1, 1].wait_recv()
        twin_send(half)
        yield
        for made in twin:
            made.wait_recv()
        yield

    def at_y(k):
        return lax.rem(a + (k + N_Y), N_Y)

    def at_x(k):
        return lax.rem(b + (k + N_X), N_X)

    def probe_path():
        for m in range(whole_probe.shape[0] + 1):
            swap(m).wait_recv()
            w.started.append(swap(m))
        r0[...] += sums[:, :, :, :, :, lanes]
        first = []
        for k in range(1, N_Y):
            first.append((0, k, w.start(r0.at[:, at_y(k), :, 0], pa.at[0, k - 1], w.slot(), {"ty": at_y(k)})))
        for k in range(1, N_X):
            first.append((1, k, w.start(r0.at[:, :, at_x(k), 1], pa.at[1, k - 1], w.slot(), {"tx": at_x(k)})))
        yield
        q[0] = r0[:, a, :, 0]
        q[1] = r0[:, :, b, 1]
        for i, k, made in first:
            made.wait_recv()
            q[i] += pa[i, k - 1]
        second = []
        for k in range(1, N_X):
            second.append((0, k, w.start(q.at[0, :, at_x(k)], pb.at[0, k - 1], w.slot(), {"tx": at_x(k)})))
        for k in range(1, N_Y):
            second.append((1, k, w.start(q.at[1, :, at_y(k)], pb.at[1, k - 1], w.slot(), {"ty": at_y(k)})))
        yield
        tt[:, 0] = q[0, :, b]
        tt[:, 1] = q[1, :, a]
        for i, k, made in second:
            made.wait_recv()
            tt[:, i] += pb[i, k - 1]
        st[:, 0] = tt[0:8]
        for k in range(nz):
            st[k, 1] = tt[8]
        third = [w.start(st.at[zat(k)], pz.at[k - 1], w.slot(), zdev(k)) for k in range(1, nz)]
        yield
        whole = st[z]
        for k in range(1, nz):
            third[k - 1].wait_recv()
            whole = whole + pz[k - 1]
        loads[1].wait()
        pout[z, a, b, :, :, lanes] = probe[...] + whole[0] / (whole[1] + 1.0)
        spot = pout.at[z, a, b, :, :, lanes]
        fourth = [w.start(spot, spot, w.slot(), zdev(k)) for k in range(1, nz)]
        yield
        for made in fourth:
            made.wait_recv()
        fifth = []
        spot = pout.at[:, a, b, 0, :, lanes]
        for k in range(1, N_X):
            fifth.append(w.start(spot, spot, w.slot(), {"tx": at_x(k)}))
        spot = pout.at[:, a, b, 1, :, lanes]
        for k in range(1, N_Y):
            fifth.append(w.start(spot, spot, w.slot(), {"ty": at_y(k)}))
        yield
        for made in fifth:
            made.wait_recv()
        sixth, pairs = [], []
        spot = pout.at[:, a, :, 0, :, lanes]
        for k in range(1, N_Y):
            sixth.append((w.start(spot, spot, w.slot(), {"ty": at_y(k)}), pout.at[:, at_y(-k), :, 0, :, lanes]))
        pairs.append(w.start(spot, spot, w.slot(), sib))
        spot = pout.at[:, :, b, 1, :, lanes]
        for k in range(1, N_X):
            sixth.append((w.start(spot, spot, w.slot(), {"tx": at_x(k)}), pout.at[:, :, at_x(-k), 1, :, lanes]))
        pairs.append(w.start(spot, spot, w.slot(), sib))
        yield
        for k in (0, 3, 2, 5, 1, 4):
            made, spot = sixth[k]
            made.wait_recv()
            pairs.append(w.start(spot, spot, w.slot(), sib))
        yield
        for made in pairs:
            made.wait_recv()
        yield

    objects, probes = object_path(), probe_path()
    for turn in MERGE_ORDER:
        next({"o": objects, "p": probes}[turn])
    for path in (objects, probes):
        for _ in path:
            pass
    w.finish()


MERGE_ORDER = "opooopopopoopopooopop"
WIRES = 190


def step_call(offs, obj, probe, amps, live):
    channels = 2
    vm = pl.BlockSpec(memory_space=pltpu.VMEM)
    far = pl.BlockSpec(memory_space=pl.ANY)
    nz = N_POS // 2
    g = 5 * channels
    half = nz // 2
    modes = probe.shape[0]
    consts = [jnp.asarray(x) for x in tables()]

    def v(*shape):
        return pltpu.VMEM(shape, f32)

    out, pout = pl.pallas_call(
        step_kernel,
        out_shape=(
            jax.ShapeDtypeStruct((2, 3, N_POS, 8, TILE), f32),
            jax.ShapeDtypeStruct((8, N_Y, N_X, 2, 8, N), f32),
        ),
        in_specs=[pl.BlockSpec(memory_space=pltpu.SMEM)] + [far] * 6,
        out_specs=(vm, vm),
        scratch_shapes=[
            v(2, EXT, EXT), pltpu.VMEM((4, N_POS, 1, 128), jnp.int32), pltpu.SMEM((4, N_POS, 1, 128), jnp.int32),
            v(*probe.shape), v(*amps.shape), pltpu.VMEM((N, N), jnp.int32), pltpu.VMEM((6, N, N), bf16), v(4, H, H),
            v(2, N, N), v(modes, 2, N, N), v(2, H, N), v(2, N, N), v(N, N),
            v(g, nz, 2, 8, EXT), v(9, N_Y, N_X, 2, 8, N),
            v(2, 3, 8, TILE), v(2, 8, 128), pltpu.VMEM((3, N, N), bf16),
            v(48 * N_POS, N), v(48 * N_POS, N), v(24, TILE),
            v(nz, g, 8, EXT), v(half, g, 8, EXT), v(half, g, 8, EXT), v(channels, 5, 8, EXT),
            v(channels, 3, 8, N), v(channels, 2, 8, TILE), v(channels, 2, 8, N), v(channels, 3, 8, TILE),
            v(2, 3, 8, EXT), v(2, 3, 8, 128), v(2, 3, 8, 128),
            v(8, TILE), v(8, TILE), v(8, EXT), v(8, EXT), v(8, EXT), v(8, EXT),
            v(9, N_Y, N_X, 2, 8, 128), v(2, 3, 9, 4, 8, 128), v(2, 9, 4, 8, 128), v(2, 3, 9, 8, 128),
            v(9, 2, 8, 128), v(8, 2, 2, 8, 128), v(7, 2, 2, 8, 128),
            pltpu.SemaphoreType.DMA((9,)), pltpu.SemaphoreType.DMA((WIRES,)), pltpu.SemaphoreType.DMA((WIRES,)),
        ],
        compiler_params=pltpu.CompilerParams(collective_id=0, has_side_effects=True, vmem_limit_bytes=60 * 2**20),
        name="step",
    )(offs, obj.reshape(2, 3, N_POS, 8, TILE), probe.reshape(8, N_Y, N_X, 2, 8, N), amps, live, *consts)
    return out.reshape(2, TILE, TILE), pout.reshape(probe.shape)


def body(object_field, probe, amplitudes, live_pixels, offsets):
    return step_call(offsets, object_field, probe, amplitudes, live_pixels)


def solution(mesh):
    return jax.shard_map(
        body,
        mesh=mesh,
        in_specs=(
            P(None, "ty", "tx"),
            P(),
            P(("pos", "ty", "tx"), None, None),
            P(),
            P(("pos", "ty", "tx"), None),
        ),
        out_specs=(P(None, "ty", "tx"), P()),
        check_vma=False,
    )
```

```python
import functools, math
import numpy as np, ml_dtypes
import jax, jax.numpy as jnp
from jax import lax
from jax.experimental import pallas as pl
from jax.experimental.pallas import tpu as pltpu
from jax.sharding import PartitionSpec as P

N = 256
H = 128
TILE = 384
EXT = 640
intensity_floor = 0.25
flux_floor = 0.25
tv_weight = 0.1
N_POS, N_Y, N_X = 16, 4, 4
f32, bf16 = jnp.float32, jnp.bfloat16


def tables():
    k = np.arange(H)
    ang = 2.0 * np.pi * ((k[:, None] * k[None, :]) % H) / H
    c, s = np.cos(ang) / 16.0, np.sin(ang) / 16.0
    m = np.block([[c, -s], [s, c]]).astype(np.float32)
    hi = m.astype(ml_dtypes.bfloat16)
    lo = (m - hi.astype(np.float32)).astype(ml_dtypes.bfloat16)
    th = 2.0 * np.pi * k / N
    tw = np.stack([np.cos(th), np.sin(th)]).astype(np.float32)
    turns = np.stack([np.tile(tw[0][:, None], (1, H)), np.tile(tw[1][:, None], (1, H)),
                      np.tile(tw[0], (H, 1)), np.tile(tw[1], (H, 1))])
    perm = np.concatenate([np.arange(0, N, 2), np.arange(1, N, 2)])
    pick = np.zeros((N, N), np.float32)
    pick[np.arange(N), perm] = 1.0
    pick = pick.astype(ml_dtypes.bfloat16)
    return np.stack([hi, lo, hi.T, lo.T, pick, pick.T]), turns


def split(x):
    hi = x.astype(bf16)
    lo = (x - hi.astype(f32)).astype(bf16)
    return hi, lo


def over(hi, lo):
    return jnp.concatenate([hi, hi, lo], 0)


def beside(hi, lo):
    return jnp.concatenate([hi, hi, lo], 1)


def right(x, table):
    hi, lo = split(x)
    return jnp.dot(jnp.concatenate([hi, lo, hi], 1), table, preferred_element_type=f32)


def left(table, x):
    hi, lo = split(x)
    return jnp.dot(table, jnp.concatenate([hi, lo, hi], 0), preferred_element_type=f32)


def split_dot_l(p, x):
    hi, lo = split(x)
    return jnp.dot(p, hi, preferred_element_type=f32) + jnp.dot(p, lo, preferred_element_type=f32)


def split_dot_r(x, p):
    hi, lo = split(x)
    return jnp.dot(hi, p, preferred_element_type=f32) + jnp.dot(lo, p, preferred_element_type=f32)


def shift_up_left(x, srow, scol):
    lane = lax.broadcasted_iota(jnp.int32, (N + 8, 128), 1)
    back = lax.rem(128 - scol, 128)
    turned = [pltpu.roll(x[:, 128 * i:128 * (i + 1)], back, 1) for i in range(3)]
    keep = lane < 128 - scol
    x = jnp.concatenate([jnp.where(keep, turned[i], turned[i + 1]) for i in range(2)], 1)
    x = x.reshape(N // 8 + 1, 8, N)
    x = pltpu.roll(x, lax.rem(8 - srow, 8), 1)
    sub = lax.broadcasted_iota(jnp.int32, (N // 8, 8, N), 1)
    return jnp.where(sub < 8 - srow, x[:-1], x[1:]).reshape(N, N)


def shift_down_right(x, srow, scol):
    x = pltpu.roll(x.reshape(N // 8, 8, N), srow, 1)
    none = jnp.zeros((1, 8, N), f32)
    sub = lax.broadcasted_iota(jnp.int32, (N // 8 + 1, 8, N), 1)
    x = jnp.where(sub >= srow, jnp.concatenate([x, none], 0), jnp.concatenate([none, x], 0))
    x = x.reshape(N + 8, N)
    lane = lax.broadcasted_iota(jnp.int32, (N + 8, 128), 1)
    t = [pltpu.roll(x[:, 128 * i:128 * (i + 1)], scol, 1) for i in range(2)]
    keep = lane >= scol
    return jnp.concatenate([jnp.where(keep, t[0], 0.0), jnp.where(keep, t[1], t[0]), jnp.where(keep, 0.0, t[1])], 1)


STRIDES = ((32, 64), (16, 48), (8, 40), (4, 36), (2, 34), (1, 33))


def bit_of(x, bit):
    return lax.rem(lax.div(x, bit), 2) == 1


def cut_window(ext, c, row, col):
    row8, u = lax.div(row, 8), lax.div(col, 128)
    blocks = [ext[c, :, 128 * i:128 * (i + 1)].reshape(EXT // 8, 8, 128) for i in range(5)]
    out = []
    for o in range(3):
        v = jnp.where(u == 0, blocks[o], jnp.where(u == 1, blocks[o + 1], blocks[o + 2]))
        for bit, size in STRIDES:
            if bit == 32:
                v = jnp.concatenate([jnp.where(bit_of(row8, bit), v[32:80], v[0:48]), v[48:64]], 0)
            else:
                v = jnp.where(bit_of(row8, bit), v[bit:bit + size], v[:size])
        out.append(v.reshape(N + 8, 128))
    return shift_up_left(jnp.concatenate(out, 1), row - 8 * row8, col - 128 * u)


def add_window(frame, c, x, row, col):
    row8, u = lax.div(row, 8), lax.div(col, 128)
    moved = shift_down_right(x, row - 8 * row8, col - 128 * u)
    placed = []
    for o in range(3):
        v = moved[:, 128 * o:128 * (o + 1)].reshape(N // 8 + 1, 8, 128)
        for bit in (1, 2, 4, 8, 16):
            none = jnp.zeros((bit, 8, 128), f32)
            v = jnp.where(bit_of(row8, bit), jnp.concatenate([none, v], 0), jnp.concatenate([v, none], 0))
        none = jnp.zeros((32, 8, 128), f32)
        v = jnp.where(bit_of(row8, 32), jnp.concatenate([none, v[:48]], 0), jnp.concatenate([v, none[:16]], 0))
        placed.append(v)
    none = jnp.zeros((EXT // 8, 8, 128), f32)

    def at(k):
        return placed[k] if 0 <= k < 3 else none

    for o in range(5):
        v = jnp.where(u == 0, at(o), jnp.where(u == 1, at(o - 1), at(o - 2)))
        frame[5 * c:5 * c + 5, :, :, :, 128 * o:128 * (o + 1)] += v.reshape(5, *frame.shape[1:4], 128)


def prepare(live, probe, squares, mask, wparts):
    power = jnp.zeros((N, N), f32)
    for m in range(probe.shape[0]):
        power = power + (probe[m, 0] * probe[m, 0] + probe[m, 1] * probe[m, 1])
    for i in range(3):
        wparts[i] = power.astype(bf16)
        power = power - wparts[i].astype(f32)
    on = (live[...] == 1).astype(bf16)
    on = jnp.dot(squares[4], on, preferred_element_type=f32).astype(bf16)
    mask[...] = jnp.dot(on, squares[5], preferred_element_type=f32)


def visit_positions(slots, offs, ext, probe, amps, squares, turns, frame, sums, patch, far, fac, grad, mask, hand_over):
    modes = probe.shape[0]
    split_rows = sums.shape[1:]

    @pl.loop(0, slots)
    def _(p):
        row = offs[p, 0] - TILE * lax.axis_index("ty")
        col = offs[p, 1] - TILE * lax.axis_index("tx")
        for c in range(2):
            patch[c] = cut_window(ext, c, row, col)
        pr, pi = patch[0], patch[1]
        sums[2 * modes] += (pr * pr + pi * pi).reshape(split_rows)

        @pl.when(p == slots - 1)
        def _():
            hand_over(modes)

        grad[...] = jnp.zeros_like(grad)
        fac[...] = jnp.zeros_like(fac)

        @pl.loop(0, modes, unroll=4)
        def _(m):
            pr, pi = patch[0], patch[1]
            qr, qi = probe[m, 0], probe[m, 1]
            wr = qr * pr - qi * pi
            wi = qr * pi + qi * pr
            ar, ai = wr[:, :H] + wr[:, H:], wi[:, :H] + wi[:, H:]
            br, bi = wr[:, :H] - wr[:, H:], wi[:, :H] - wi[:, H:]
            tc, ts = turns[2, 0:1], turns[3, 0:1]
            br, bi = br * tc + bi * ts, bi * tc - br * ts
            even = right(jnp.concatenate([ar, ai], 1), over(squares[0], squares[1]))
            odd = right(jnp.concatenate([br, bi], 1), over(squares[0], squares[1]))
            total = None
            rc, rs = turns[0], turns[1]
            for h, z in enumerate((even, odd)):
                zr, zi = z[:, :H], z[:, H:]
                ar, ai = zr[:H] + zr[H:], zi[:H] + zi[H:]
                br, bi = zr[:H] - zr[H:], zi[:H] - zi[H:]
                br, bi = br * rc + bi * rs, bi * rc - br * rs
                both = jnp.concatenate([jnp.concatenate([ar, br], 1), jnp.concatenate([ai, bi], 1)], 0)
                out = left(beside(squares[2], squares[3]), both)
                far[m, h] = out
                sq = out * out
                power = sq[:H] + sq[H:]
                fac[h] += power

        amp = split_dot_r(split_dot_l(squares[4], amps[p]), squares[5])
        for h in range(2):
            want = jnp.concatenate([amp[:H, h * H:(h + 1) * H], amp[H:, h * H:(h + 1) * H]], 1)
            lv = jnp.concatenate([mask[:H, h * H:(h + 1) * H], mask[H:, h * H:(h + 1) * H]], 1)
            fac[h] = jnp.where(lv > 0.5, want * lax.rsqrt(jnp.maximum(fac[h], intensity_floor)), 1.0)

        for m in range(modes):
            rc, rs = turns[0], turns[1]
            halves = []
            for h in range(2):
                f = far[m, h]
                k = fac[h]
                y = jnp.concatenate([f[:H] * k, f[H:] * k], 0)
                x = left(beside(squares[0], squares[1]), y)
                er, orr = x[:H, :H], x[:H, H:]
                ei, oi = x[H:, :H], x[H:, H:]
                orr, oi = orr * rc - oi * rs, oi * rc + orr * rs
                top = jnp.concatenate([er + orr, ei + oi], 1)
                bottom = jnp.concatenate([er - orr, ei - oi], 1)
                halves.append(right(jnp.concatenate([top, bottom], 0), over(squares[2], squares[3])))
            e, o = halves
            er, ei, orr, oi = e[:, :H], e[:, H:], o[:, :H], o[:, H:]
            tc, ts = turns[2, 0:1], turns[3, 0:1]
            orr, oi = orr * tc - oi * ts, oi * tc + orr * ts
            nr = jnp.concatenate([er + orr, er - orr], 1)
            ni = jnp.concatenate([ei + oi, ei - oi], 1)
            pr, pi = patch[0], patch[1]
            qr, qi = probe[m, 0], probe[m, 1]
            dr = nr - (qr * pr - qi * pi)
            di = ni - (qr * pi + qi * pr)
            grad[0] += qr * dr + qi * di
            grad[1] += qr * di - qi * dr
            sums[2 * m] += (pr * dr + pi * di).reshape(split_rows)
            sums[2 * m + 1] += (pr * di - pi * dr).reshape(split_rows)

            @pl.when(p == slots - 1)
            def _():
                hand_over(m)

        for c in range(2):
            add_window(frame, c, grad[c], row, col)


MESH = pl.DeviceIdType.MESH


class Wires:
    def __init__(self, send, recv):
        self.send, self.recv, self.count, self.started = send, recv, 0, []

    def slot(self):
        self.count += 1
        return self.count - 1

    def copy(self, src, dst, slot, to):
        return pltpu.make_async_remote_copy(
            src_ref=src, dst_ref=dst, send_sem=self.send.at[slot], recv_sem=self.recv.at[slot],
            device_id=to, device_id_type=MESH)

    def start(self, src, dst, slot, to):
        made = self.copy(src, dst, slot, to)
        made.start()
        self.started.append(made)
        return made

    def finish(self):
        for made in self.started:
            made.wait_send()


def greet(partners):
    barrier = pltpu.get_barrier_semaphore()
    for to in partners:
        pl.semaphore_signal(barrier, inc=1, device_id=to, device_id_type=MESH)
    pl.semaphore_wait(barrier, len(partners))


def places():
    p = lax.axis_index("pos")
    return p, p // 2, lax.rem(p, 2), lax.axis_index("ty"), lax.axis_index("tx")


SHARED = 4


def gather_halo(w, offs, obj, ext, table, here, ready):
    p, z, c, a, b = places()
    nz = N_POS // 2
    tile = obj.shape[1]
    up, down = lax.rem(a + N_Y - 1, N_Y), lax.rem(a + 1, N_Y)
    left, right_ = lax.rem(b + N_X - 1, N_X), lax.rem(b + 1, N_X)
    after, before = {"pos": 2 * lax.rem(z + 1, nz) + c}, {"pos": 2 * lax.rem(z + nz - 1, nz) + c}
    sib = {"pos": 2 * z + 1 - c}
    odd = lax.rem(z, 2)
    group = [{"pos": lax.rem(p + k, N_POS)} for k in range(1, N_POS)]
    own = pltpu.make_async_copy(obj, ext.at[:, 0:tile, 0:tile], here)
    own.start()

    def spans(e, k):
        if k == SHARED:
            return pl.ds(256, 128), pl.ds(192, 64)
        return (pl.ds(pl.multiple_of(128 * e + 32 * k, 8), 32), pl.ds(pl.multiple_of(96 * e + 24 * k, 8), 24))

    def lower(rows):
        return pl.ds(pl.multiple_of(tile + rows.start, 8), rows.size)

    def rims(e, k):
        side, below = spans(e, k)
        return ext.at[c, side, tile:tile + N], ext.at[c, lower(below), :]

    came = []

    def push(k):
        side, below = spans(odd, k)
        came.append((
            w.start(obj.at[c, side, 0:N], ext.at[c, side, tile:tile + N], w.slot(), {"tx": left}),
            w.start(obj.at[c, below, :], ext.at[c, lower(below), 0:tile], w.slot(), {"ty": up}),
            w.start(obj.at[c, below, 0:N], ext.at[c, lower(below), tile:tile + N], w.slot(), {"ty": up, "tx": left}),
        ))

    push(0)
    for k in range(1, SHARED):
        push(k)
    lane = lax.broadcasted_iota(jnp.int32, (1, 128), 1)
    row = jnp.zeros((1, 128), jnp.int32)
    for i in range(2 * offs.shape[0]):
        row = jnp.where(lane == i, offs[i // 2, i % 2], row)
    table[0, p] = row
    line = table.at[0, p]
    lines = [w.start(line, line, w.slot(), to) for to in group]
    ready()
    pair, relay = [], []
    for k in range(SHARED + 1):
        for made in came[k]:
            made.wait_recv()
        if k == 1:
            push(SHARED)
        for spot in rims(odd, k):
            if k < SHARED:
                relay.append(w.start(spot, spot, w.slot(), after if k % 2 == 0 else before))
        for spot in rims(odd, k):
            pair.append(w.start(spot, spot, w.slot(), sib))
        if k == 1:
            for made in lines:
                made.wait_recv()
            for t, to in ((1, {"ty": down}), (2, {"tx": right_}), (3, {"ty": down, "tx": right_})):
                pair.append(w.start(table.at[0], table.at[t], w.slot(), to))
    for k in range(SHARED):
        for i, spot in enumerate(rims(1 - odd, k)):
            relay[2 * k + i].wait_recv()
            pair.append(w.start(spot, spot, w.slot(), sib))
    for made in pair:
        made.wait_recv()
    own.wait()


def step_kernel(offs, obj_far, probe_far, amps_far, live_far, squares_far, turns_far, out, pout,
                ext, table, offs_all, whole_probe, amps, live, squares, turns, patch, far, fac, grad, mask,
                frame, sums, obj, probe, wparts, hot, rows_of, wsum,
                s, rin, lin, t, fr, fb, fc, acc, wide, hl, hr, tops, bots, up_in, up_edge, dn_in, dn_edge,
                r0, pa, q, pb, tt, st, pz, here, send, recv):
    channels = 2
    p, z, c, a, b = places()
    lanes = pl.ds(pl.multiple_of(c * 128, 128), 128)
    others = pl.ds(pl.multiple_of((1 - c) * 128, 128), 128)
    loads = [pltpu.make_async_copy(src, dst, here.at[i]) for i, (src, dst) in enumerate((
        (obj_far.at[:, :, p], obj), (probe_far.at[z, a, b, :, :, lanes], probe),
        (probe_far.reshape(whole_probe.shape), whole_probe), (squares_far, squares), (turns_far, turns),
        (live_far, live), (amps_far, amps)))]
    for load in loads:
        load.start()
    nz = N_POS // 2
    half = nz // 2
    up, down = lax.rem(a + N_Y - 1, N_Y), lax.rem(a + 1, N_Y)
    left, right_ = lax.rem(b + N_X - 1, N_X), lax.rem(b + 1, N_X)
    following, previous = lax.rem(p + 1, N_POS), lax.rem(p + N_POS - 1, N_POS)

    def zat(k):
        return lax.rem(z + (k + nz), nz)

    def zdev(k):
        return {"pos": 2 * zat(k) + c}

    sib = {"pos": 2 * z + 1 - c}
    for ref in (tops, bots, up_in, up_edge, dn_in, dn_edge):
        ref[...] = jnp.zeros_like(ref)
    greet([{"ty": lax.rem(a + k, N_Y)} for k in range(1, N_Y)]
          + [{"tx": lax.rem(b + k, N_X)} for k in range(1, N_X)]
          + [{"ty": down, "tx": right_}, {"ty": up, "tx": left}]
          + [{"pos": lax.rem(p + k, N_POS)} for k in range(1, N_POS)]
          + [{"pos": N_POS - 1 - p, "ty": down}, {"pos": N_POS - 1 - p, "ty": up}]
          + [{"pos": N_POS - 1 - p, "ty": down, "tx": left}, {"pos": N_POS - 1 - p, "ty": up, "tx": right_}]
          + [{"pos": following, "tx": left}, {"pos": previous, "tx": right_}])
    w = Wires(send, recv)

    def ready():
        for ref in (frame, sums, wsum):
            ref[...] = jnp.zeros_like(ref)
        for load in loads[2:]:
            load.wait()
        prepare(live, whole_probe, squares, mask, wparts)

    gather_halo(w, offs, obj_far.reshape(2, TILE, TILE), ext, table, here.at[7], ready)
    swap_slots = [w.slot() for _ in range(whole_probe.shape[0] + 1)]

    def swap(m):
        two = pl.ds(2 * m, 2 if m < whole_probe.shape[0] else 1)
        return w.copy(sums.at[two, :, :, :, :, others], r0.at[two], swap_slots[m], sib)

    known = pltpu.make_async_copy(table, offs_all, here.at[8])
    known.start()
    visit_positions(amps.shape[0], offs, ext, whole_probe, amps, squares, turns, frame, sums,
                    patch, far, fac, grad, mask, lambda m: swap(m).start())
    known.wait()
    spread = lax.broadcasted_iota(jnp.int32, (8, N), 1) - lax.broadcasted_iota(jnp.int32, (8, N), 0)
    lane = lax.broadcasted_iota(jnp.int32, (24, 128), 1)

    def weigh(which):
        @pl.loop(0, 2 * N_POS)
        def _(i):
            row = offs_all[which, lax.div(i, 2), 0, 2 * lax.rem(i, 2)] - TILE * a
            for g in range(3):
                first = (g * N_POS + p) * 8 - row
                hot[pl.ds(pl.multiple_of(24 * i + 8 * g, 8), 8), :] = jnp.where(spread == first, 1.0, 0.0)

        pick = hot[...].astype(bf16)
        rows_of[...] = (jnp.dot(pick, wparts[0], preferred_element_type=f32)
                        + jnp.dot(pick, wparts[1], preferred_element_type=f32)
                        + jnp.dot(pick, wparts[2], preferred_element_type=f32))

        def one(i, carry):
            col = offs_all[which, lax.div(i, 2), 0, 2 * lax.rem(i, 2) + 1] - TILE * b
            col = jnp.clip(col + TILE, 0, 2 * TILE)
            u = lax.div(col, 128)
            s_ = col - 128 * u
            u = u - 3
            x = rows_of[pl.ds(pl.multiple_of(24 * i, 8), 24), :]
            t0, t1 = pltpu.roll(x[:, :128], s_, 1), pltpu.roll(x[:, 128:], s_, 1)
            keep = lane >= s_
            g0, g1, g2 = jnp.where(keep, t0, 0.0), jnp.where(keep, t1, t0), jnp.where(keep, 0.0, t1)
            return tuple(
                carry[o] + jnp.where(u == o, g0, jnp.where(u == o - 1, g1, jnp.where(u == o - 2, g2, 0.0)))
                for o in range(3))

        zero = jnp.zeros((24, 128), f32)
        added = lax.fori_loop(0, 2 * N_POS, one, (zero,) * 3, unroll=4)
        wsum[...] += jnp.concatenate(added, 1)

    total = frame.shape[0]
    cut = (total + 1) // 2
    parts = (pl.ds(0, cut), pl.ds(cut, total - cut))

    def object_path():
        order = [half]
        for k in range(half - 1, 0, -1):
            order += [k, -k]
        order += [0]
        swaps = {}

        def swap_more(count):
            for k in order[len(swaps):len(swaps) + count]:
                swaps[k] = w.start(frame.at[:, zat(k), 1 - c], s.at[zat(k)], w.slot(), sib)

        swap_more(3)
        yield

        def mine(k):
            swaps[k].wait_recv()
            s[zat(k)] += frame[:, zat(k), c]

        went = {}
        for step in range(half):
            for k in ((half,) if step == 0 else (half - step, step - half)):
                mine(k)
            for part in range(2):
                for way, box in ((1, rin), (-1, lin)):
                    if step == 0 and part != (0 if way == 1 else 1):
                        continue
                    d = zat(way * (half - step))
                    before = went.get((step - 1, way, part))
                    if before is not None:
                        before.wait_recv()
                        s[d, parts[part]] += box[step - 1, parts[part]]
                    went[step, way, part] = w.start(
                        s.at[d, parts[part]], box.at[step, parts[part]], w.slot(), zdev(way))
            swap_more(3)
            weigh(step)
            yield
        mine(0)
        last = half - 1
        for part in range(2):
            for way, box in ((1, rin), (-1, lin)):
                went[last, way, part].wait_recv()
                s[z, parts[part]] += box[last, parts[part]]
        t[...] = s[z].reshape(channels, 5, 8, EXT)
        f1 = w.start(t.at[:, 0:3, :, TILE:EXT], fr, w.slot(), {"tx": right_})
        f2 = w.start(t.at[:, 3:5, :, 0:TILE], fb, w.slot(), {"ty": down})
        f3 = w.start(t.at[:, 3:5, :, TILE:EXT], fc, w.slot(), {"ty": down, "tx": right_})
        yield
        acc[...] = t[:, 0:3, :, 0:TILE]
        f1.wait_recv()
        acc[:, :, :, 0:N] += fr[...]
        f2.wait_recv()
        acc[:, 0:2] += fb[...]
        f3.wait_recv()
        acc[:, 0:2, :, 0:N] += fc[...]
        share = wsum[...].reshape(3, 8, TILE) + 1.0
        loads[0].wait()
        for ch in range(2):
            wide[ch, :, :, 128:128 + TILE] = obj[ch] + acc[ch] / share
        h1 = w.start(wide.at[:, :, :, TILE:TILE + 128], hl, w.slot(), {"tx": right_})
        h2 = w.start(wide.at[:, :, :, 128:256], hr, w.slot(), {"tx": left})
        for ch in range(2):
            for g in range(3):
                k = 3 * ch + g
                tops[k:k + 1, :] = wide[ch, g, 0:1, 128:128 + TILE]
                bots[k:k + 1, :] = wide[ch, g, 7:8, 128:128 + TILE]
        inner, first, final = pl.ds(128, TILE), pl.ds(0, 128), pl.ds(128 + TILE, 128)
        rows_sent = [
            w.start(bots, up_in.at[:, inner], w.slot(), {"pos": following}),
            w.start(tops, dn_in.at[:, inner], w.slot(), {"pos": previous}),
            w.start(bots.at[:, 0:128], up_in.at[:, final], w.slot(), {"pos": following, "tx": left}),
            w.start(tops.at[:, TILE - 128:TILE], dn_in.at[:, first], w.slot(), {"pos": previous, "tx": right_}),
        ]
        k3 = [w.slot(), w.slot()]
        k4 = [w.slot(), w.slot()]

        def last_down():
            return [w.copy(bots, up_edge.at[:, inner], k3[0], {"pos": 0, "ty": down}),
                    w.copy(bots.at[:, 0:128], up_edge.at[:, final], k3[1], {"pos": 0, "ty": down, "tx": left})]

        def first_up():
            return [w.copy(tops, dn_edge.at[:, inner], k4[0], {"pos": N_POS - 1, "ty": up}),
                    w.copy(tops.at[:, TILE - 128:TILE], dn_edge.at[:, first], k4[1],
                           {"pos": N_POS - 1, "ty": up, "tx": right_})]

        @pl.when(p == N_POS - 1)
        def _():
            for made in last_down():
                made.start()

        @pl.when(p == 0)
        def _():
            for made in first_up():
                made.start()

        yield
        h1.wait_recv()
        wide[:, :, :, 0:128] = jnp.where(b > 0, hl[...], 0.0)
        h2.wait_recv()
        wide[:, :, :, 128 + TILE:] = jnp.where(b < N_X - 1, hr[...], 0.0)
        for made in rows_sent:
            made.wait_recv()

        @pl.when(p == 0)
        def _():
            for made in last_down():
                made.wait_recv()
            for made in first_up():
                made.wait_send()

        @pl.when(p == N_POS - 1)
        def _():
            for made in first_up():
                made.wait_recv()
            for made in last_down():
                made.wait_send()

        in_left = lax.broadcasted_iota(jnp.int32, (1, EXT), 1) >= jnp.where(b > 0, 0, 128)
        in_right = lax.broadcasted_iota(jnp.int32, (1, EXT), 1) < jnp.where(b < N_X - 1, EXT, 128 + TILE)
        sub = lax.broadcasted_iota(jnp.int32, (8, EXT), 0)

        def unit(x, below):
            fx = [pltpu.roll(v, EXT - 1, 1) - v for v in x]
            fy = [n - v for v, n in zip(x, below)]
            power = fx[0] * fx[0] + fy[0] * fy[0] + fx[1] * fx[1] + fy[1] * fy[1]
            mag = jnp.sqrt(jnp.maximum(power, flux_floor))
            return [v / mag for v in fx], [v / mag for v in fy]

        for g in range(3):
            x, above, below = [], [], []
            for ch in range(2):
                k = 3 * ch + g
                v = wide[ch, g]
                if g == 0:
                    edge = jnp.where(a > 0, up_edge[3 * ch + 2:3 * ch + 3, :], 0.0)
                else:
                    edge = up_in[k - 1:k, :]
                first = jnp.where(in_right, jnp.where(p == 0, edge, up_in[k:k + 1, :]), 0.0)
                if g == 2:
                    edge = jnp.where(a < N_Y - 1, dn_edge[3 * ch:3 * ch + 1, :], 0.0)
                else:
                    edge = dn_in[k + 1:k + 2, :]
                final = jnp.where(in_left, jnp.where(p == N_POS - 1, edge, dn_in[k:k + 1, :]), 0.0)
                x.append(v)
                above.append(jnp.where(sub == 0, first, pltpu.roll(v, 1, 0)))
                below.append(jnp.where(sub == 7, final, pltpu.roll(v, 7, 0)))
            nx, ny = unit(x, below)
            _, my = unit(above, x)
            for ch in range(2):
                div = nx[ch] - pltpu.roll(nx[ch], 1, 1) + ny[ch] - my[ch]
                out[ch, g, p] = (x[ch] + tv_weight * div)[:, 128:128 + TILE]
        went, twin = {}, []

        def twin_send(k):
            q_ = 2 * zat(k) + c
            twin.append(w.start(out.at[:, :, q_], out.at[:, :, q_], w.slot(), sib))

        for step in range(half):
            for way in (1, -1):
                q_ = 2 * zat(-way * step) + c
                for ch in range(2):
                    if step == half - 1 and ch != (0 if way == 1 else 1):
                        continue
                    if step > 0:
                        went[step - 1, way, ch].wait_recv()
                    went[step, way, ch] = w.start(out.at[ch, :, q_], out.at[ch, :, q_], w.slot(), zdev(way))
                if step == half - 1:
                    went[step - 1, way, 1 if way == 1 else 0].wait_recv()
                if step == 0:
                    if way == 1:
                        twin_send(0)
                else:
                    twin_send(-way * step)
            yield
        went[half - 1, 1, 0].wait_recv()
        went[half - 1, -1, 1].wait_recv()
        twin_send(half)
        yield
        for made in twin:
            made.wait_recv()
        yield

    def at_y(k):
        return lax.rem(a + (k + N_Y), N_Y)

    def at_x(k):
        return lax.rem(b + (k + N_X), N_X)

    def probe_path():
        for m in range(whole_probe.shape[0] + 1):
            swap(m).wait_recv()
            w.started.append(swap(m))
        r0[...] += sums[:, :, :, :, :, lanes]
        first = []
        for k in range(1, N_Y):
            first.append((0, k, w.start(r0.at[:, at_y(k), :, 0], pa.at[0, k - 1], w.slot(), {"ty": at_y(k)})))
        for k in range(1, N_X):
            first.append((1, k, w.start(r0.at[:, :, at_x(k), 1], pa.at[1, k - 1], w.slot(), {"tx": at_x(k)})))
        yield
        q[0] = r0[:, a, :, 0]
        q[1] = r0[:, :, b, 1]
        for i, k, made in first:
            made.wait_recv()
            q[i] += pa[i, k - 1]
        second = []
        for k in range(1, N_X):
            second.append((0, k, w.start(q.at[0, :, at_x(k)], pb.at[0, k - 1], w.slot(), {"tx": at_x(k)})))
        for k in range(1, N_Y):
            second.append((1, k, w.start(q.at[1, :, at_y(k)], pb.at[1, k - 1], w.slot(), {"ty": at_y(k)})))
        yield
        tt[:, 0] = q[0, :, b]
        tt[:, 1] = q[1, :, a]
        for i, k, made in second:
            made.wait_recv()
            tt[:, i] += pb[i, k - 1]
        st[:, 0] = tt[0:8]
        for k in range(nz):
            st[k, 1] = tt[8]
        third = [w.start(st.at[zat(k)], pz.at[k - 1], w.slot(), zdev(k)) for k in range(1, nz)]
        yield
        whole = st[z]
        for k in range(1, nz):
            third[k - 1].wait_recv()
            whole = whole + pz[k - 1]
        loads[1].wait()
        pout[z, a, b, :, :, lanes] = probe[...] + whole[0] / (whole[1] + 1.0)
        spot = pout.at[z, a, b, :, :, lanes]
        fourth = [w.start(spot, spot, w.slot(), zdev(k)) for k in range(1, nz)]
        yield
        for made in fourth:
            made.wait_recv()
        fifth = []
        spot = pout.at[:, a, b, 0, :, lanes]
        for k in range(1, N_X):
            fifth.append(w.start(spot, spot, w.slot(), {"tx": at_x(k)}))
        spot = pout.at[:, a, b, 1, :, lanes]
        for k in range(1, N_Y):
            fifth.append(w.start(spot, spot, w.slot(), {"ty": at_y(k)}))
        yield
        for made in fifth:
            made.wait_recv()
        sixth, pairs = [], []
        spot = pout.at[:, a, :, 0, :, lanes]
        for k in range(1, N_Y):
            sixth.append((w.start(spot, spot, w.slot(), {"ty": at_y(k)}), pout.at[:, at_y(-k), :, 0, :, lanes]))
        pairs.append(w.start(spot, spot, w.slot(), sib))
        spot = pout.at[:, :, b, 1, :, lanes]
        for k in range(1, N_X):
            sixth.append((w.start(spot, spot, w.slot(), {"tx": at_x(k)}), pout.at[:, :, at_x(-k), 1, :, lanes]))
        pairs.append(w.start(spot, spot, w.slot(), sib))
        yield
        for k in (0, 3, 2, 5, 1, 4):
            made, spot = sixth[k]
            made.wait_recv()
            pairs.append(w.start(spot, spot, w.slot(), sib))
        yield
        for made in pairs:
            made.wait_recv()
        yield

    objects, probes = object_path(), probe_path()
    for turn in MERGE_ORDER:
        next({"o": objects, "p": probes}[turn])
    for path in (objects, probes):
        for _ in path:
            pass
    w.finish()


MERGE_ORDER = "opoopoopopoopopooopop"
WIRES = 190


def step_call(offs, obj, probe, amps, live):
    channels = 2
    vm = pl.BlockSpec(memory_space=pltpu.VMEM)
    far = pl.BlockSpec(memory_space=pl.ANY)
    nz = N_POS // 2
    g = 5 * channels
    half = nz // 2
    modes = probe.shape[0]
    consts = [jnp.asarray(x) for x in tables()]

    def v(*shape):
        return pltpu.VMEM(shape, f32)

    out, pout = pl.pallas_call(
        step_kernel,
        out_shape=(
            jax.ShapeDtypeStruct((2, 3, N_POS, 8, TILE), f32),
            jax.ShapeDtypeStruct((8, N_Y, N_X, 2, 8, N), f32),
        ),
        in_specs=[pl.BlockSpec(memory_space=pltpu.SMEM)] + [far] * 6,
        out_specs=(vm, vm),
        scratch_shapes=[
            v(2, EXT, EXT), pltpu.VMEM((4, N_POS, 1, 128), jnp.int32), pltpu.SMEM((4, N_POS, 1, 128), jnp.int32),
            v(*probe.shape), v(*amps.shape), pltpu.VMEM((N, N), jnp.int32), pltpu.VMEM((6, N, N), bf16), v(4, H, H),
            v(2, N, N), v(modes, 2, N, N), v(2, H, N), v(2, N, N), v(N, N),
            v(g, nz, 2, 8, EXT), v(9, N_Y, N_X, 2, 8, N),
            v(2, 3, 8, TILE), v(2, 8, 128), pltpu.VMEM((3, N, N), bf16),
            v(48 * N_POS, N), v(48 * N_POS, N), v(24, TILE),
            v(nz, g, 8, EXT), v(half, g, 8, EXT), v(half, g, 8, EXT), v(channels, 5, 8, EXT),
            v(channels, 3, 8, N), v(channels, 2, 8, TILE), v(channels, 2, 8, N), v(channels, 3, 8, TILE),
            v(2, 3, 8, EXT), v(2, 3, 8, 128), v(2, 3, 8, 128),
            v(8, TILE), v(8, TILE), v(8, EXT), v(8, EXT), v(8, EXT), v(8, EXT),
            v(9, N_Y, N_X, 2, 8, 128), v(2, 3, 9, 4, 8, 128), v(2, 9, 4, 8, 128), v(2, 3, 9, 8, 128),
            v(9, 2, 8, 128), v(8, 2, 2, 8, 128), v(7, 2, 2, 8, 128),
            pltpu.SemaphoreType.DMA((9,)), pltpu.SemaphoreType.DMA((WIRES,)), pltpu.SemaphoreType.DMA((WIRES,)),
        ],
        compiler_params=pltpu.CompilerParams(collective_id=0, has_side_effects=True, vmem_limit_bytes=60 * 2**20),
        name="step",
    )(offs, obj.reshape(2, 3, N_POS, 8, TILE), probe.reshape(8, N_Y, N_X, 2, 8, N), amps, live, *consts)
    return out.reshape(2, TILE, TILE), pout.reshape(probe.shape)


def body(object_field, probe, amplitudes, live_pixels, offsets):
    return step_call(offsets, object_field, probe, amplitudes, live_pixels)


def solution(mesh):
    return jax.shard_map(
        body,
        mesh=mesh,
        in_specs=(
            P(None, "ty", "tx"),
            P(),
            P(("pos", "ty", "tx"), None, None),
            P(),
            P(("pos", "ty", "tx"), None),
        ),
        out_specs=(P(None, "ty", "tx"), P()),
        check_vma=False,
    )
```
